256 devices in a mesh: grp: 8 (over x_hi, y), freq: 32 (over x_lo, z, core).
Axes of the slice: x: 4 (x_hi: 2, x_lo: 2; x = x_hi * 2 + x_lo), y: 4, z: 8, core: 2. Of those that a mesh axis runs over, the one named last changes fastest.
Arguments:
- residuals: bfloat16 [64, 32, 2, 4096], P('grp', None, None, 'freq'), may hold values from -6 to 6
- system_matrix: bfloat16 [4096, 2, 16384], P('freq'), may hold values from -0.0625 to 0.0625
- offsets: int32 [64], replicated, may hold values from 0 to 31
- patch_ids: int32 [64], replicated, may hold values from 0 to 63, each once
Outputs:
- volume: float32 [32, 2, 32, 16384], P(None, None, 'grp', 'freq')
The draws below stay inside these ranges and needn't reach their ends.
All inputs are finite; a program needn't handle non-finite values.
Results may differ from the reference program's by a relative error of at most 0.0003.
Values may be sent and summed in bfloat16 or wider, within the bound.
No kernel may reach another device: no remote copies, remote signals or barrier semaphores. Data moves between devices by JAX's collectives and lax.ppermute only.
A program may use at most 192 MiB of HBM per device.

```python
import math
import jax
import jax.numpy as jnp
import numpy as np
from jax import lax

F = 4096
BRICK = 16384
FRAMES = 32
P_SIZE = 64
NBRICK = 32


def plant(values, own_key, smallest, largest):
    longest = values.shape.index(max(values.shape))
    spots = []
    for shift in (0, 1):
        where = [jax.random.randint(jax.random.fold_in(own_key, axis), (), 0, length) for axis, length in enumerate(values.shape)]
        where[longest] = (where[longest] + shift) % values.shape[longest]
        spots.append(tuple(where))
    return values.at[spots[0]].set(smallest).at[spots[1]].set(largest)


def levels(own_key, dims, pieces, least, top_value):
    gain = 1.0
    for dim, parts in pieces:
        heights = jax.random.uniform(jax.random.fold_in(jax.random.fold_in(own_key, 6), dim), (parts,), jnp.float32, least / len(pieces), top_value / len(pieces))
        gain = gain * jnp.repeat(jnp.exp(heights), dims[dim] // parts).reshape((-1,) + (1,) * (len(dims) - 1 - dim))
    return gain


def rank_table(number_of, lean):
    loads = [(1 << 20) // math.isqrt(standing ** lean) + 1 for standing in range(1, number_of + 1)]
    scale = 1 + sum(loads) // (1 << 30)
    return np.cumsum(np.array([max(1, weight // scale) for weight in loads]))


def ranked(key, dims, amount, slope):
    grid = rank_table(amount, slope)
    lot = jax.random.randint(jax.random.fold_in(key, 1), dims, 0, int(grid[amount - 1]))
    rank = jnp.searchsorted(jnp.asarray(grid, jnp.int32), lot, side="right")
    return jax.random.permutation(jax.random.fold_in(key, 2), amount)[rank].astype(jnp.int32)


def centred(own_key, extent, width, limit, cuts=(), kind=jnp.bfloat16):
    array = width * jax.random.normal(own_key, extent, jnp.float32)
    if cuts:
        array = array * levels(own_key, extent, cuts, -0.22, 0.18)
    return jnp.clip(array, -limit, limit).astype(kind)


def setup_inputs(seed: int = 0) -> dict:
    splits = jax.random.split(jax.random.key(seed), 5)
    return {
        "residuals": centred(splits[0], (P_SIZE, FRAMES, 2, F), 1.0, 6.0, ((0, 8), (3, 32))),
        "system_matrix": centred(splits[1], (F, 2, BRICK), (2 * F) ** -0.5, 0.0625, ((0, 32),)),
        "offsets": plant(ranked(splits[2], (P_SIZE,), NBRICK, 2), jax.random.fold_in(splits[2], 3), 0, NBRICK - 1).astype(jnp.int32),
        "patch_ids": jax.random.permutation(splits[3], P_SIZE).astype(jnp.int32),
    }


def reference(residuals, system_matrix, offsets, patch_ids):
    resid = residuals.astype(jnp.float32)
    matrix = system_matrix.astype(jnp.float32)
    high = lax.Precision.HIGHEST
    real_part = jnp.einsum("ptf,fv->ptv", resid[:, :, 0], matrix[:, 0], precision=high) + jnp.einsum("ptf,fv->ptv", resid[:, :, 1], matrix[:, 1], precision=high)
    imag_part = jnp.einsum("ptf,fv->ptv", resid[:, :, 1], matrix[:, 0], precision=high) - jnp.einsum("ptf,fv->ptv", resid[:, :, 0], matrix[:, 1], precision=high)
    slab_terms = jnp.stack([real_part, imag_part], axis=2)
    targets = offsets[patch_ids].astype(jnp.int32)
    bricks = jnp.arange(NBRICK, dtype=jnp.int32)
    select = (targets[:, None] == bricks[None, :]).astype(jnp.float32)
    return jnp.einsum("pk,ptcv->tckv", select, slab_terms, precision=high)
```

```python
import functools

import jax
import jax.numpy as jnp
from jax import lax
from jax.experimental import pallas as pl
from jax.experimental.pallas import tpu as pltpu
from jax.sharding import PartitionSpec as P

XH, Y, XL, Z, CORE = 2, 4, 2, 8, 2
NX = XH * XL
BR_DEV = 4
TARGETS = (4, -3, 3, -2, 2, -1, 1, 0)
MESSAGES = ((0, 1), (2,), (3,), (4,), (5,), (6,), (7,))
FREE = pl.CostEstimate(flops=1000, bytes_accessed=1000, transcendentals=0)
PARAMS = pltpu.CompilerParams(vmem_limit_bytes=24 * 2**20)
SMEM = pl.BlockSpec(memory_space=pltpu.SMEM)
VMEM = pl.BlockSpec(memory_space=pltpu.VMEM)
F32, BF16 = jnp.float32, jnp.bfloat16


def linear(xh, y, xl, z, c):
    return (((xh * Y + y) * XL + xl) * Z + z) * CORE + c


def shift(array, dx=0, dy=0, dz=0, dc=0, mirror=False):
    pairs = []
    for x in range(NX):
        for y in range(Y):
            for z in range(Z):
                for c in range(CORE):
                    way = -1 if mirror and c else 1
                    tx = (x + way * dx) % NX
                    ty, tz, t = (y + way * dy) % Y, (z + way * dz) % Z, (c + dc) % CORE
                    pairs.append((linear(x // 2, y, x % 2, z, c), linear(tx // 2, ty, tx % 2, tz, t)))
    return lax.ppermute(array, ("grp", "freq"), pairs)


def place():
    grp, freq = lax.axis_index("grp"), lax.axis_index("freq")
    return grp >> 2, grp & 3, freq >> 4, (freq >> 1) & 7, freq & 1


def add_rows_kernel(place_ref, offs_ref, ids_ref, r0, r1, r2, r3, same, plus, minus, other, acc):
    xh, y, xl = place_ref[0], place_ref[1], place_ref[2]
    rows = r0.shape[0]
    acc[...] = jnp.zeros_like(acc)
    for dy, ref in enumerate((r0, r1, r2, r3)):
        first = (xh * Y + (y + dy) % Y) * rows
        for i in range(rows):
            brick = offs_ref[ids_ref[first + i]]
            owner = brick // BR_DEV
            slot = (owner // Y) * BR_DEV + brick % BR_DEV
            slot = jnp.where(owner % Y == y, slot, XH * BR_DEV)
            acc[slot] += ref[i].astype(F32)
    here, there = pl.ds(xh * BR_DEV, BR_DEV), pl.ds((1 - xh) * BR_DEV, BR_DEV)
    same[...] = acc[here]
    other[...] = acc[there]
    right = jnp.where(xl == 0, xh, 1 - xh)
    plus[...] = acc[pl.ds(right * BR_DEV, BR_DEV)]
    minus[...] = acc[pl.ds((1 - right) * BR_DEV, BR_DEV)]


def add_rows(where, offsets, patch_ids, pieces):
    tc, width = pieces[0].shape[1:]
    out = jax.ShapeDtypeStruct((BR_DEV, tc, width), F32)
    return pl.pallas_call(
        add_rows_kernel,
        out_shape=[out] * 4,
        in_specs=[SMEM] * 3 + [VMEM] * 4,
        out_specs=[VMEM] * 4,
        compiler_params=PARAMS,
        cost_estimate=FREE,
        scratch_shapes=[pltpu.VMEM((XH * BR_DEV + 1, tc, width), F32)],
        name="add_rows",
    )(where, offsets, patch_ids, *pieces)


def expand_kernel(a0, a1, b0, b1, out):
    bricks, tc, width = a0.shape
    rows, depth = bricks * tc, 2 * width
    r = lax.broadcasted_iota(jnp.int32, (rows, rows), 0)
    s = lax.broadcasted_iota(jnp.int32, (rows, rows), 1)
    reorder = (s == (r % bricks) * tc + r // bricks).astype(F32).astype(BF16)
    f = lax.broadcasted_iota(jnp.int32, (depth, depth), 0)
    k = lax.broadcasted_iota(jnp.int32, (depth, depth), 1)
    weave = (k == 2 * (f % width) + f // width).astype(F32).astype(BF16)
    part = lax.broadcasted_iota(jnp.int32, (rows, width), 0) % 2
    dot = functools.partial(jnp.dot, preferred_element_type=F32)
    parts = []
    for u, v in ((a0, a1), (b0, b1)):
        x = (u[...] + v[...]).reshape(rows, width)
        xs = jnp.where(part == 0, pltpu.roll(x, rows - 1, 0), -pltpu.roll(x, 1, 0))
        both = jnp.concatenate([x, xs], axis=1)
        hi = both.astype(BF16)
        parts += [hi, (both - hi.astype(F32)).astype(BF16)]
    woven = dot(jnp.concatenate(parts, axis=0), weave).astype(BF16)
    wide = jnp.concatenate([woven[i * rows:(i + 1) * rows] for i in range(4)], axis=1)
    wide = dot(reorder, wide).astype(BF16)
    for i in range(4):
        out[i // 2, i % 2] = wide[:, i * depth:(i + 1) * depth]


def expand(a0, a1, b0, b1):
    bricks, tc, width = a0.shape
    rows = bricks * tc
    return pl.pallas_call(
        expand_kernel,
        out_shape=jax.ShapeDtypeStruct((2, 2, rows, 2 * width), BF16),
        in_specs=[VMEM] * 4,
        out_specs=VMEM,
        compiler_params=PARAMS,
        cost_estimate=FREE,
        name="expand",
    )(a0, a1, b0, b1)


def cut_matrix(where, matrix, messages, room, local=False):
    width, parts, voxels = matrix.shape
    span = voxels // (XL * Z * CORE)
    piece = (width, parts, span)
    shapes = [(2, len(message)) + piece for message in messages] + [(Z,) + piece] * (2 * local)
    count = 2 * sum(map(len, messages)) + 2 * Z * local

    def kernel(place_ref, src, *rest):
        outs, sems = rest[:-1], rest[-1]
        xl, z, c = place_ref[2], place_ref[3], place_ref[4]
        wanted = [
            (s, 1, dc, out.at[dc, k]) for out, message in zip(outs, messages) for k, s in enumerate(message) for dc in range(2)
        ]
        if local:
            wanted += [(s, 0, dc, outs[dc - 2].at[s]) for s in range(Z) for dc in range(2)]
        copies = []
        for i, (s, dxl, dc, out) in enumerate(wanted):
            reader = (c + dc) % CORE
            at = (z + Z + (1 - 2 * reader) * TARGETS[s]) % Z
            first = (((xl + dxl) % XL * Z + at) * CORE + reader) * span
            columns = src.at[:, :, pl.ds(pl.multiple_of(first, span), span)]
            copies.append(pltpu.make_async_copy(columns, out, sems.at[i]))
        for copy in copies:
            copy.start()
        for copy in copies:
            copy.wait()

    return pl.pallas_call(
        kernel,
        in_specs=[SMEM, pl.BlockSpec(memory_space=pltpu.HBM)],
        out_specs=[VMEM] * len(shapes),
        out_shape=[jax.ShapeDtypeStruct(s, BF16) for s in shapes],
        scratch_shapes=[pltpu.SemaphoreType.DMA((count,))],
        compiler_params=pltpu.CompilerParams(vmem_limit_bytes=room * 2**20),
        cost_estimate=FREE,
        name="cut_matrix",
    )(where, matrix)


def flatten_kernel(i, k, own, core, far, cross, out):
    for n, m in enumerate((own.at[i], core.at[i], far.at[0, k], cross.at[k])):
        out[n] = m[...].reshape(out.shape[1:])


def flatten(own, core, far, cross, i, k):
    width, parts, span = own.shape[1:]
    return pl.pallas_call(
        functools.partial(flatten_kernel, i, k),
        out_shape=jax.ShapeDtypeStruct((4, width * parts, span), BF16),
        in_specs=[VMEM] * 4,
        out_specs=VMEM,
        compiler_params=PARAMS,
        cost_estimate=FREE,
        name="flatten",
    )(own, core, far, cross)


def term_kernel(el, ec, flat, *rest):
    dot = functools.partial(jnp.dot, preferred_element_type=F32)
    total = None if len(rest) == 1 else rest[0][...]
    for n, e in enumerate((el.at[0], ec.at[0], el.at[1], ec.at[1])):
        for h in range(2):
            d = dot(e[h], flat[n])
            total = d if total is None else total + d
    rest[-1][...] = total


def term(el, ec, flat, *so_far):
    return pl.pallas_call(
        term_kernel,
        out_shape=jax.ShapeDtypeStruct((el.shape[2], flat.shape[2]), F32),
        in_specs=[VMEM] * (3 + len(so_far)),
        out_specs=VMEM,
        compiler_params=PARAMS,
        cost_estimate=FREE,
        name="term",
    )(el, ec, flat, *so_far)


def finish_kernel(a, b, c, out):
    out[...] = (a[...] + b[...] + c[...]).reshape(out.shape)


def finish(*parts):
    rows, cols = parts[0].shape
    return pl.pallas_call(
        finish_kernel,
        out_shape=jax.ShapeDtypeStruct((rows // BR_DEV, BR_DEV, cols), F32),
        in_specs=[VMEM] * 3,
        out_specs=VMEM,
        compiler_params=PARAMS,
        cost_estimate=FREE,
        name="finish",
    )(*parts)


def on_device(residuals, system_matrix, offsets, patch_ids):
    xh, y, xl, z, c = place()
    where = jnp.stack([xh, y, xl, z, c]).astype(jnp.int32)
    rows, frames, parts, width = residuals.shape
    tc = frames * parts
    raw = residuals.reshape(rows, tc, width)
    pieces = [shift(raw, dy=-1), shift(raw, dy=2), shift(raw, dy=1)]
    (far,) = cut_matrix(where, system_matrix, MESSAGES[:1], 56)
    fars = [across(far)]
    matrix, pieces[0] = lax.optimization_barrier((system_matrix, pieces[0]))
    *far, own, core = cut_matrix(where, matrix, MESSAGES[1:], 48, local=True)
    sent = add_rows(where, offsets, patch_ids, [raw] + pieces)
    (same, plus, minus, other), fars[0], core = lax.optimization_barrier((sent, fars[0], core))
    rest = [shift(plus, dx=1), shift(minus, dx=-1), shift(other, dx=2)]
    core = shift(core, dc=1)
    cross = shift(fars[0][1], dc=1)
    flats = [flatten(own, core, fars[0], cross, s, s) for s in MESSAGES[0]]
    far[0], flats, rest = lax.optimization_barrier((far[0], flats, rest))
    fars.append(across(far[0]))
    from_left, from_right, across_two = rest
    el = expand(same, across_two, from_left, from_right)
    far[1], el = lax.optimization_barrier((far[1], el))
    fars.append(across(far[1]))
    ec = shift(el, dc=1)

    sums = [None, None]
    for s in range(Z):
        if s >= 2:
            fars[s - 1], total = lax.optimization_barrier((fars[s - 1], total))
            sums[1 - s % 2] = shift(total, dz=2 * (s % 2) - 1, mirror=True)
            cross = shift(fars[s - 1][1], dc=1)
            flats.append(flatten(own, core, fars[s - 1], cross, s, 0))
        if s == Z - 1:
            total = term(el, ec, flats[s])
            break
        total = term(el, ec, flats[s], *sums[s % 2:s % 2 + 1] if s > 1 else ())
        if s == 0:
            flats[1], total = lax.optimization_barrier((flats[1], total))
            sums[0] = shift(total, dz=1, mirror=True)
        if 1 <= s < Z - 3:
            late, total = lax.optimization_barrier((far[s + 1], total))
            fars.append(across(late))
    volume = finish(total, *sums)
    return volume.reshape(frames, parts, BR_DEV, -1)


def across(far):
    return shift(far, dx=1, mirror=True)


def solution(mesh):
    in_specs = (P("grp", None, None, "freq"), P("freq", None, None), P(), P())
    out_specs = P(None, None, "grp", "freq")
    return jax.shard_map(
        on_device, mesh=mesh, in_specs=in_specs, out_specs=out_specs, check_vma=False
    )
```

```python
import functools

import jax
import jax.numpy as jnp
from jax import lax
from jax.experimental import pallas as pl
from jax.experimental.pallas import tpu as pltpu
from jax.sharding import PartitionSpec as P

XH, Y, XL, Z, CORE = 2, 4, 2, 8, 2
NX = XH * XL
BR_DEV = 4
TARGETS = (4, -3, 3, -2, 2, -1, 1, 0)
MESSAGES = ((0, 1), (2,), (3,), (4,), (5,), (6,), (7,))
PACE = (1, 2, 3)
FREE = pl.CostEstimate(flops=1000, bytes_accessed=1000, transcendentals=0)
PARAMS = pltpu.CompilerParams(vmem_limit_bytes=24 * 2**20)
SMEM = pl.BlockSpec(memory_space=pltpu.SMEM)
VMEM = pl.BlockSpec(memory_space=pltpu.VMEM)
F32, BF16 = jnp.float32, jnp.bfloat16


def linear(xh, y, xl, z, c):
    return (((xh * Y + y) * XL + xl) * Z + z) * CORE + c


def shift(array, dx=0, dy=0, dz=0, dc=0, mirror=False):
    pairs = []
    for x in range(NX):
        for y in range(Y):
            for z in range(Z):
                for c in range(CORE):
                    way = -1 if mirror and c else 1
                    tx = (x + way * dx) % NX
                    ty, tz, t = (y + way * dy) % Y, (z + way * dz) % Z, (c + dc) % CORE
                    pairs.append((linear(x // 2, y, x % 2, z, c), linear(tx // 2, ty, tx % 2, tz, t)))
    return lax.ppermute(array, ("grp", "freq"), pairs)


def place():
    grp, freq = lax.axis_index("grp"), lax.axis_index("freq")
    return grp >> 2, grp & 3, freq >> 4, (freq >> 1) & 7, freq & 1


def add_rows_kernel(place_ref, offs_ref, ids_ref, r0, r1, r2, r3, same, plus, minus, other, acc):
    xh, y, xl = place_ref[0], place_ref[1], place_ref[2]
    rows = r0.shape[0]
    acc[...] = jnp.zeros_like(acc)
    for dy, ref in enumerate((r0, r1, r2, r3)):
        first = (xh * Y + (y + dy) % Y) * rows
        for i in range(rows):
            brick = offs_ref[ids_ref[first + i]]
            owner = brick // BR_DEV
            slot = (owner // Y) * BR_DEV + brick % BR_DEV
            slot = jnp.where(owner % Y == y, slot, XH * BR_DEV)
            acc[slot] += ref[i].astype(F32)
    here, there = pl.ds(xh * BR_DEV, BR_DEV), pl.ds((1 - xh) * BR_DEV, BR_DEV)
    same[...] = acc[here]
    other[...] = acc[there]
    right = jnp.where(xl == 0, xh, 1 - xh)
    plus[...] = acc[pl.ds(right * BR_DEV, BR_DEV)]
    minus[...] = acc[pl.ds((1 - right) * BR_DEV, BR_DEV)]


def add_rows(where, offsets, patch_ids, pieces):
    tc, width = pieces[0].shape[1:]
    out = jax.ShapeDtypeStruct((BR_DEV, tc, width), F32)
    return pl.pallas_call(
        add_rows_kernel,
        out_shape=[out] * 4,
        in_specs=[SMEM] * 3 + [VMEM] * 4,
        out_specs=[VMEM] * 4,
        compiler_params=PARAMS,
        cost_estimate=FREE,
        scratch_shapes=[pltpu.VMEM((XH * BR_DEV + 1, tc, width), F32)],
        name="add_rows",
    )(where, offsets, patch_ids, *pieces)


def expand_kernel(a0, a1, b0, b1, out):
    bricks, tc, width = a0.shape
    rows, depth = bricks * tc, 2 * width
    r = lax.broadcasted_iota(jnp.int32, (rows, rows), 0)
    s = lax.broadcasted_iota(jnp.int32, (rows, rows), 1)
    reorder = (s == (r % bricks) * tc + r // bricks).astype(F32).astype(BF16)
    f = lax.broadcasted_iota(jnp.int32, (depth, depth), 0)
    k = lax.broadcasted_iota(jnp.int32, (depth, depth), 1)
    weave = (k == 2 * (f % width) + f // width).astype(F32).astype(BF16)
    part = lax.broadcasted_iota(jnp.int32, (rows, width), 0) % 2
    dot = functools.partial(jnp.dot, preferred_element_type=F32)
    parts = []
    for u, v in ((a0, a1), (b0, b1)):
        x = (u[...] + v[...]).reshape(rows, width)
        xs = jnp.where(part == 0, pltpu.roll(x, rows - 1, 0), -pltpu.roll(x, 1, 0))
        both = jnp.concatenate([x, xs], axis=1)
        hi = both.astype(BF16)
        parts += [hi, (both - hi.astype(F32)).astype(BF16)]
    woven = dot(jnp.concatenate(parts, axis=0), weave).astype(BF16)
    wide = jnp.concatenate([woven[i * rows:(i + 1) * rows] for i in range(4)], axis=1)
    wide = dot(reorder, wide).astype(BF16)
    for i in range(4):
        out[i // 2, i % 2] = wide[:, i * depth:(i + 1) * depth]


def expand(a0, a1, b0, b1):
    bricks, tc, width = a0.shape
    rows = bricks * tc
    return pl.pallas_call(
        expand_kernel,
        out_shape=jax.ShapeDtypeStruct((2, 2, rows, 2 * width), BF16),
        in_specs=[VMEM] * 4,
        out_specs=VMEM,
        compiler_params=PARAMS,
        cost_estimate=FREE,
        name="expand",
    )(a0, a1, b0, b1)


def cut_matrix(where, matrix, messages, local=False):
    width, parts, voxels = matrix.shape
    span = voxels // (XL * Z * CORE)
    piece = (width, parts, span)
    shapes = [(2, len(message)) + piece for message in messages] + [(Z,) + piece] * (2 * local)
    count = 2 * sum(map(len, messages)) + 2 * Z * local

    def kernel(place_ref, src, *rest):
        outs, sems = rest[:-1], rest[-1]
        xl, z, c = place_ref[2], place_ref[3], place_ref[4]
        wanted = [
            (s, 1, dc, out.at[dc, k]) for out, message in zip(outs, messages) for k, s in enumerate(message) for dc in range(2)
        ]
        if local:
            wanted += [(s, 0, dc, outs[dc - 2].at[s]) for s in range(Z) for dc in range(2)]
        copies = []
        for i, (s, dxl, dc, out) in enumerate(wanted):
            reader = (c + dc) % CORE
            at = (z + Z + (1 - 2 * reader) * TARGETS[s]) % Z
            first = (((xl + dxl) % XL * Z + at) * CORE + reader) * span
            columns = src.at[:, :, pl.ds(pl.multiple_of(first, span), span)]
            copies.append(pltpu.make_async_copy(columns, out, sems.at[i]))
        for copy in copies:
            copy.start()
        for copy in copies:
            copy.wait()

    return pl.pallas_call(
        kernel,
        in_specs=[SMEM, pl.BlockSpec(memory_space=pltpu.HBM)],
        out_specs=[VMEM] * len(shapes),
        out_shape=[jax.ShapeDtypeStruct(s, BF16) for s in shapes],
        scratch_shapes=[pltpu.SemaphoreType.DMA((count,))],
        compiler_params=PARAMS,
        cost_estimate=FREE,
        name="cut_matrix",
    )(where, pltpu.with_memory_space_constraint(matrix, pltpu.HBM))


def flatten_kernel(i, k, own, core, far, cross, out):
    for n, m in enumerate((own.at[i], core.at[i], far.at[0, k], cross.at[k])):
        out[n] = m[...].reshape(out.shape[1:])


def flatten(own, core, far, cross, i, k):
    width, parts, span = own.shape[1:]
    return pl.pallas_call(
        functools.partial(flatten_kernel, i, k),
        out_shape=jax.ShapeDtypeStruct((4, width * parts, span), BF16),
        in_specs=[VMEM] * 4,
        out_specs=VMEM,
        compiler_params=PARAMS,
        cost_estimate=FREE,
        name="flatten",
    )(own, core, far, cross)


def term_kernel(el, ec, flat, *rest):
    dot = functools.partial(jnp.dot, preferred_element_type=F32)
    total = None if len(rest) == 1 else rest[0][...]
    for n, e in enumerate((el.at[0], ec.at[0], el.at[1], ec.at[1])):
        for h in range(2):
            d = dot(e[h], flat[n])
            total = d if total is None else total + d
    rest[-1][...] = total


def term(el, ec, flat, *so_far):
    return pl.pallas_call(
        term_kernel,
        out_shape=jax.ShapeDtypeStruct((el.shape[2], flat.shape[2]), F32),
        in_specs=[VMEM] * (3 + len(so_far)),
        out_specs=VMEM,
        compiler_params=PARAMS,
        cost_estimate=FREE,
        name="term",
    )(el, ec, flat, *so_far)


def finish_kernel(a, b, c, out):
    out[...] = (a[...] + b[...] + c[...]).reshape(out.shape)


def finish(*parts):
    rows, cols = parts[0].shape
    return pl.pallas_call(
        finish_kernel,
        out_shape=jax.ShapeDtypeStruct((rows // BR_DEV, BR_DEV, cols), F32),
        in_specs=[VMEM] * 3,
        out_specs=VMEM,
        compiler_params=PARAMS,
        cost_estimate=FREE,
        name="finish",
    )(*parts)


def on_device(residuals, system_matrix, offsets, patch_ids):
    xh, y, xl, z, c = place()
    where = jnp.stack([xh, y, xl, z, c]).astype(jnp.int32)
    rows, frames, parts, width = residuals.shape
    tc = frames * parts
    raw = residuals.reshape(rows, tc, width)
    pieces = [shift(raw, dy=-1), shift(raw, dy=2), shift(raw, dy=1)]
    (far,) = cut_matrix(where, system_matrix, MESSAGES[:1])
    fars = [across(far)]
    matrix, pieces[0] = lax.optimization_barrier((system_matrix, pieces[0]))
    *far, own, core = cut_matrix(where, matrix, MESSAGES[1:], local=True)
    sent = add_rows(where, offsets, patch_ids, [raw] + pieces)
    (same, plus, minus, other), fars[0], core = lax.optimization_barrier((sent, fars[0], core))
    rest = [shift(plus, dx=1), shift(minus, dx=-1), shift(other, dx=2)]
    core = shift(core, dc=1)
    cross = shift(fars[0][1], dc=1)
    flats = [flatten(own, core, fars[0], cross, s, s) for s in MESSAGES[0]]
    for i in range(3):
        far[i], rest[i] = lax.optimization_barrier((far[i], rest[i]))
        fars.append(across(far[i]))
    flats, rest = lax.optimization_barrier((flats, rest))
    from_left, from_right, across_two = rest
    el = expand(same, across_two, from_left, from_right)
    ec = shift(el, dc=1)

    sums = [None, None]
    for s in range(Z):
        if s >= 2:
            fars[s - 1], total = lax.optimization_barrier((fars[s - 1], total))
            sums[1 - s % 2] = shift(total, dz=2 * (s % 2) - 1, mirror=True)
            cross = shift(fars[s - 1][1], dc=1)
            flats.append(flatten(own, core, fars[s - 1], cross, s, 0))
        if s == Z - 1:
            total = term(el, ec, flats[s])
            break
        total = term(el, ec, flats[s], *sums[s % 2:s % 2 + 1] if s > 1 else ())
        if s in PACE:
            late, total = lax.optimization_barrier((far[len(fars) - 1], total))
            fars.append(across(late))
        if s == 0:
            flats[1], total = lax.optimization_barrier((flats[1], total))
            sums[0] = shift(total, dz=1, mirror=True)
    volume = finish(total, *sums)
    return volume.reshape(frames, parts, BR_DEV, -1)


def across(far):
    return shift(far, dx=1, mirror=True)


def solution(mesh):
    in_specs = (P("grp", None, None, "freq"), P("freq", None, None), P(), P())
    out_specs = P(None, None, "grp", "freq")
    return jax.shard_map(
        on_device, mesh=mesh, in_specs=in_specs, out_specs=out_specs, check_vma=False
    )
```

```python
import functools

import jax
import jax.numpy as jnp
from jax import lax
from jax.experimental import pallas as pl
from jax.experimental.pallas import tpu as pltpu
from jax.sharding import PartitionSpec as P

XH, Y, XL, Z, CORE = 2, 4, 2, 8, 2
NX = XH * XL
BR_DEV = 4
TARGETS = (4, -3, 3, -2, 2, -1, 1, 0)
MESSAGES = ((0, 1), (2,), (3,), (4,), (5,), (6,), (7,))
PACE = (1, 2, 3)
FREE = pl.CostEstimate(flops=1000, bytes_accessed=1000, transcendentals=0)
PARAMS = pltpu.CompilerParams(vmem_limit_bytes=24 * 2**20)
SMEM = pl.BlockSpec(memory_space=pltpu.SMEM)
VMEM = pl.BlockSpec(memory_space=pltpu.VMEM)
F32, BF16 = jnp.float32, jnp.bfloat16


def linear(xh, y, xl, z, c):
    return (((xh * Y + y) * XL + xl) * Z + z) * CORE + c


def shift(array, dx=0, dy=0, dz=0, dc=0, mirror=False):
    pairs = []
    for x in range(NX):
        for y in range(Y):
            for z in range(Z):
                for c in range(CORE):
                    way = -1 if mirror and c else 1
                    tx = (x + way * dx) % NX
                    ty, tz, t = (y + way * dy) % Y, (z + way * dz) % Z, (c + dc) % CORE
                    pairs.append((linear(x // 2, y, x % 2, z, c), linear(tx // 2, ty, tx % 2, tz, t)))
    return lax.ppermute(array, ("grp", "freq"), pairs)


def place():
    grp, freq = lax.axis_index("grp"), lax.axis_index("freq")
    return grp >> 2, grp & 3, freq >> 4, (freq >> 1) & 7, freq & 1


def add_rows_kernel(place_ref, offs_ref, ids_ref, r0, r1, r2, r3, same, plus, minus, other, acc):
    xh, y, xl = place_ref[0], place_ref[1], place_ref[2]
    rows = r0.shape[0]
    acc[...] = jnp.zeros_like(acc)
    for dy, ref in enumerate((r0, r1, r2, r3)):
        first = (xh * Y + (y + dy) % Y) * rows
        for i in range(rows):
            brick = offs_ref[ids_ref[first + i]]
            owner = brick // BR_DEV
            slot = (owner // Y) * BR_DEV + brick % BR_DEV
            slot = jnp.where(owner % Y == y, slot, XH * BR_DEV)
            acc[slot] += ref[i].astype(F32)
    here, there = pl.ds(xh * BR_DEV, BR_DEV), pl.ds((1 - xh) * BR_DEV, BR_DEV)
    same[...] = acc[here]
    other[...] = acc[there]
    right = jnp.where(xl == 0, xh, 1 - xh)
    plus[...] = acc[pl.ds(right * BR_DEV, BR_DEV)]
    minus[...] = acc[pl.ds((1 - right) * BR_DEV, BR_DEV)]


def add_rows(where, offsets, patch_ids, pieces):
    tc, width = pieces[0].shape[1:]
    out = jax.ShapeDtypeStruct((BR_DEV, tc, width), F32)
    return pl.pallas_call(
        add_rows_kernel,
        out_shape=[out] * 4,
        in_specs=[SMEM] * 3 + [VMEM] * 4,
        out_specs=[VMEM] * 4,
        compiler_params=PARAMS,
        cost_estimate=FREE,
        scratch_shapes=[pltpu.VMEM((XH * BR_DEV + 1, tc, width), F32)],
        name="add_rows",
    )(where, offsets, patch_ids, *pieces)


def expand_kernel(a0, a1, b0, b1, out):
    bricks, tc, width = a0.shape
    rows, depth = bricks * tc, 2 * width
    r = lax.broadcasted_iota(jnp.int32, (rows, rows), 0)
    s = lax.broadcasted_iota(jnp.int32, (rows, rows), 1)
    reorder = (s == (r % bricks) * tc + r // bricks).astype(F32).astype(BF16)
    f = lax.broadcasted_iota(jnp.int32, (depth, depth), 0)
    k = lax.broadcasted_iota(jnp.int32, (depth, depth), 1)
    weave = (k == 2 * (f % width) + f // width).astype(F32).astype(BF16)
    part = lax.broadcasted_iota(jnp.int32, (rows, width), 0) % 2
    dot = functools.partial(jnp.dot, preferred_element_type=F32)
    parts = []
    for u, v in ((a0, a1), (b0, b1)):
        x = (u[...] + v[...]).reshape(rows, width)
        xs = jnp.where(part == 0, pltpu.roll(x, rows - 1, 0), -pltpu.roll(x, 1, 0))
        both = jnp.concatenate([x, xs], axis=1)
        hi = both.astype(BF16)
        parts += [hi, (both - hi.astype(F32)).astype(BF16)]
    woven = dot(jnp.concatenate(parts, axis=0), weave).astype(BF16)
    wide = jnp.concatenate([woven[i * rows:(i + 1) * rows] for i in range(4)], axis=1)
    wide = dot(reorder, wide).astype(BF16)
    for i in range(4):
        out[i // 2, i % 2] = wide[:, i * depth:(i + 1) * depth]


def expand(a0, a1, b0, b1):
    bricks, tc, width = a0.shape
    rows = bricks * tc
    return pl.pallas_call(
        expand_kernel,
        out_shape=jax.ShapeDtypeStruct((2, 2, rows, 2 * width), BF16),
        in_specs=[VMEM] * 4,
        out_specs=VMEM,
        compiler_params=PARAMS,
        cost_estimate=FREE,
        name="expand",
    )(a0, a1, b0, b1)


def cut_matrix(where, matrix, messages, local=()):
    width, parts, voxels = matrix.shape
    span = voxels // (XL * Z * CORE)
    piece = (width, parts, span)
    shapes = [(2, len(message)) + piece for message in messages] + [(len(steps),) + piece for steps, _ in local]
    count = 2 * sum(map(len, messages)) + sum(len(steps) for steps, _ in local)

    def kernel(place_ref, src, *rest):
        outs, sems = rest[:-1], rest[-1]
        xl, z, c = place_ref[2], place_ref[3], place_ref[4]
        wanted = [
            (s, 1, dc, out.at[dc, k]) for out, message in zip(outs, messages) for k, s in enumerate(message) for dc in range(2)
        ]
        for out, (steps, dc) in zip(outs[len(messages):], local):
            wanted += [(s, 0, dc, out.at[i]) for i, s in enumerate(steps)]
        copies = []
        for i, (s, dxl, dc, out) in enumerate(wanted):
            reader = (c + dc) % CORE
            at = (z + Z + (1 - 2 * reader) * TARGETS[s]) % Z
            first = (((xl + dxl) % XL * Z + at) * CORE + reader) * span
            columns = src.at[:, :, pl.ds(pl.multiple_of(first, span), span)]
            copies.append(pltpu.make_async_copy(columns, out, sems.at[i]))
        for copy in copies:
            copy.start()
        for copy in copies:
            copy.wait()

    return pl.pallas_call(
        kernel,
        in_specs=[SMEM, pl.BlockSpec(memory_space=pltpu.HBM)],
        out_specs=[VMEM] * len(shapes),
        out_shape=[jax.ShapeDtypeStruct(s, BF16) for s in shapes],
        scratch_shapes=[pltpu.SemaphoreType.DMA((count,))],
        compiler_params=PARAMS,
        cost_estimate=FREE,
        name="cut_matrix",
    )(where, pltpu.with_memory_space_constraint(matrix, pltpu.HBM))


def flatten_kernel(index, *refs):
    out = refs[-1]
    for n, (i, ref) in enumerate(zip(index, refs)):
        out[n] = ref[i].reshape(out.shape[1:])


def flatten(*pieces):
    arrays, index = zip(*pieces)
    width, parts, span = arrays[0].shape[-3:]
    return pl.pallas_call(
        functools.partial(flatten_kernel, index),
        out_shape=jax.ShapeDtypeStruct((4, width * parts, span), BF16),
        in_specs=[VMEM] * 4,
        out_specs=VMEM,
        compiler_params=PARAMS,
        cost_estimate=FREE,
        name="flatten",
    )(*arrays)


def term_kernel(el, ec, flat, *rest):
    dot = functools.partial(jnp.dot, preferred_element_type=F32)
    total = None if len(rest) == 1 else rest[0][...]
    for n, e in enumerate((el.at[0], ec.at[0], el.at[1], ec.at[1])):
        for h in range(2):
            d = dot(e[h], flat[n])
            total = d if total is None else total + d
    rest[-1][...] = total


def term(el, ec, flat, *so_far):
    return pl.pallas_call(
        term_kernel,
        out_shape=jax.ShapeDtypeStruct((el.shape[2], flat.shape[2]), F32),
        in_specs=[VMEM] * (3 + len(so_far)),
        out_specs=VMEM,
        compiler_params=PARAMS,
        cost_estimate=FREE,
        name="term",
    )(el, ec, flat, *so_far)


def finish_kernel(a, b, c, out):
    out[...] = (a[...] + b[...] + c[...]).reshape(out.shape)


def finish(*parts):
    rows, cols = parts[0].shape
    return pl.pallas_call(
        finish_kernel,
        out_shape=jax.ShapeDtypeStruct((rows // BR_DEV, BR_DEV, cols), F32),
        in_specs=[VMEM] * 3,
        out_specs=VMEM,
        compiler_params=PARAMS,
        cost_estimate=FREE,
        name="finish",
    )(*parts)


def on_device(residuals, system_matrix, offsets, patch_ids):
    xh, y, xl, z, c = place()
    where = jnp.stack([xh, y, xl, z, c]).astype(jnp.int32)
    rows, frames, parts, width = residuals.shape
    tc = frames * parts
    raw = residuals.reshape(rows, tc, width)
    pieces = [shift(raw, dy=-1), shift(raw, dy=2), shift(raw, dy=1)]
    (far,) = cut_matrix(where, system_matrix, MESSAGES[:1])
    fars = [across(far)]
    matrix, pieces[0] = lax.optimization_barrier((system_matrix, pieces[0]))
    early, late = MESSAGES[0], range(len(MESSAGES[0]), Z)
    *far, own, core = cut_matrix(where, matrix, MESSAGES[1:2], ((early, 0), (range(Z), 1)))
    sent = add_rows(where, offsets, patch_ids, [raw] + pieces)
    (same, plus, minus, other), fars[0], core = lax.optimization_barrier((sent, fars[0], core))
    rest = [shift(plus, dx=1), shift(minus, dx=-1), shift(other, dx=2)]
    core = shift(core, dc=1)
    cross = shift(fars[0][1], dc=1)
    flats = [flatten((own, (s,)), (core, (s,)), (fars[0], (0, s)), (cross, (s,))) for s in early]
    far[0], rest[0] = lax.optimization_barrier((far[0], rest[0]))
    fars.append(across(far[0]))
    flats, rest = lax.optimization_barrier((flats, rest))
    from_left, from_right, across_two = rest
    el = expand(same, across_two, from_left, from_right)
    matrix, el = lax.optimization_barrier((matrix, el))
    ec = shift(el, dc=1)
    *more, own = cut_matrix(where, matrix, MESSAGES[2:], ((late, 0),))
    far += more
    fars += [across(f) for f in far[1:3]]

    sums = [None, None]
    for s in range(Z):
        if s >= 2:
            fars[s - 1], total = lax.optimization_barrier((fars[s - 1], total))
            sums[1 - s % 2] = shift(total, dz=2 * (s % 2) - 1, mirror=True)
            cross = shift(fars[s - 1][1], dc=1)
            flats.append(flatten((own, (s - 2,)), (core, (s,)), (fars[s - 1], (0, 0)), (cross, (0,))))
        if s == Z - 1:
            total = term(el, ec, flats[s])
            break
        total = term(el, ec, flats[s], *sums[s % 2:s % 2 + 1] if s > 1 else ())
        if s in PACE:
            ahead, total = lax.optimization_barrier((far[len(fars) - 1], total))
            fars.append(across(ahead))
        if s == 0:
            flats[1], total = lax.optimization_barrier((flats[1], total))
            sums[0] = shift(total, dz=1, mirror=True)
    volume = finish(total, *sums)
    return volume.reshape(frames, parts, BR_DEV, -1)


def across(far):
    return shift(far, dx=1, mirror=True)


def solution(mesh):
    in_specs = (P("grp", None, None, "freq"), P("freq", None, None), P(), P())
    out_specs = P(None, None, "grp", "freq")
    return jax.shard_map(
        on_device, mesh=mesh, in_specs=in_specs, out_specs=out_specs, check_vma=False
    )
```

```python
import functools

import jax
import jax.numpy as jnp
from jax import lax
from jax.experimental import pallas as pl
from jax.experimental.pallas import tpu as pltpu
from jax.sharding import PartitionSpec as P

XH, Y, XL, Z, CORE = 2, 4, 2, 8, 2
NX = XH * XL
BR_DEV = 4
TARGETS = (4, -3, 3, -2, 2, -1, 1, 0)
MESSAGES = ((0, 1), (2,), (3,), (4,), (5,), (6,), (7,))
PACE = (1, 2, 3)
FREE = pl.CostEstimate(flops=1000, bytes_accessed=1000, transcendentals=0)
PARAMS = pltpu.CompilerParams(vmem_limit_bytes=24 * 2**20)
SMEM = pl.BlockSpec(memory_space=pltpu.SMEM)
VMEM = pl.BlockSpec(memory_space=pltpu.VMEM)
F32, BF16 = jnp.float32, jnp.bfloat16


def linear(xh, y, xl, z, c):
    return (((xh * Y + y) * XL + xl) * Z + z) * CORE + c


def shift(array, dx=0, dy=0, dz=0, dc=0, mirror=False):
    pairs = []
    for x in range(NX):
        for y in range(Y):
            for z in range(Z):
                for c in range(CORE):
                    way = -1 if mirror and c else 1
                    tx = (x + way * dx) % NX
                    ty, tz, t = (y + way * dy) % Y, (z + way * dz) % Z, (c + dc) % CORE
                    pairs.append((linear(x // 2, y, x % 2, z, c), linear(tx // 2, ty, tx % 2, tz, t)))
    return lax.ppermute(array, ("grp", "freq"), pairs)


def place():
    grp, freq = lax.axis_index("grp"), lax.axis_index("freq")
    return grp >> 2, grp & 3, freq >> 4, (freq >> 1) & 7, freq & 1


def add_rows_kernel(place_ref, offs_ref, ids_ref, r0, r1, r2, r3, same, plus, minus, other, acc):
    xh, y, xl = place_ref[0], place_ref[1], place_ref[2]
    rows = r0.shape[0]
    acc[...] = jnp.zeros_like(acc)
    for dy, ref in enumerate((r0, r1, r2, r3)):
        first = (xh * Y + (y + dy) % Y) * rows
        for i in range(rows):
            brick = offs_ref[ids_ref[first + i]]
            owner = brick // BR_DEV
            slot = (owner // Y) * BR_DEV + brick % BR_DEV
            slot = jnp.where(owner % Y == y, slot, XH * BR_DEV)
            acc[slot] += ref[i].astype(F32)
    here, there = pl.ds(xh * BR_DEV, BR_DEV), pl.ds((1 - xh) * BR_DEV, BR_DEV)
    same[...] = acc[here]
    other[...] = acc[there]
    right = jnp.where(xl == 0, xh, 1 - xh)
    plus[...] = acc[pl.ds(right * BR_DEV, BR_DEV)]
    minus[...] = acc[pl.ds((1 - right) * BR_DEV, BR_DEV)]


def add_rows(where, offsets, patch_ids, pieces):
    tc, width = pieces[0].shape[1:]
    out = jax.ShapeDtypeStruct((BR_DEV, tc, width), F32)
    return pl.pallas_call(
        add_rows_kernel,
        out_shape=[out] * 4,
        in_specs=[SMEM] * 3 + [VMEM] * 4,
        out_specs=[VMEM] * 4,
        compiler_params=PARAMS,
        cost_estimate=FREE,
        scratch_shapes=[pltpu.VMEM((XH * BR_DEV + 1, tc, width), F32)],
        name="add_rows",
    )(where, offsets, patch_ids, *pieces)


def expand_kernel(a0, a1, b0, b1, out):
    bricks, tc, width = a0.shape
    rows, depth = bricks * tc, 2 * width
    r = lax.broadcasted_iota(jnp.int32, (rows, rows), 0)
    s = lax.broadcasted_iota(jnp.int32, (rows, rows), 1)
    reorder = (s == (r % bricks) * tc + r // bricks).astype(F32).astype(BF16)
    f = lax.broadcasted_iota(jnp.int32, (depth, depth), 0)
    k = lax.broadcasted_iota(jnp.int32, (depth, depth), 1)
    weave = (k == 2 * (f % width) + f // width).astype(F32).astype(BF16)
    part = lax.broadcasted_iota(jnp.int32, (rows, width), 0) % 2
    dot = functools.partial(jnp.dot, preferred_element_type=F32)
    parts = []
    for u, v in ((a0, a1), (b0, b1)):
        x = (u[...] + v[...]).reshape(rows, width)
        xs = jnp.where(part == 0, pltpu.roll(x, rows - 1, 0), -pltpu.roll(x, 1, 0))
        both = jnp.concatenate([x, xs], axis=1)
        hi = both.astype(BF16)
        parts += [hi, (both - hi.astype(F32)).astype(BF16)]
    woven = dot(jnp.concatenate(parts, axis=0), weave).astype(BF16)
    wide = jnp.concatenate([woven[i * rows:(i + 1) * rows] for i in range(4)], axis=1)
    wide = dot(reorder, wide).astype(BF16)
    for i in range(4):
        out[i // 2, i % 2] = wide[:, i * depth:(i + 1) * depth]


def expand(a0, a1, b0, b1):
    bricks, tc, width = a0.shape
    rows = bricks * tc
    return pl.pallas_call(
        expand_kernel,
        out_shape=jax.ShapeDtypeStruct((2, 2, rows, 2 * width), BF16),
        in_specs=[VMEM] * 4,
        out_specs=VMEM,
        compiler_params=PARAMS,
        cost_estimate=FREE,
        name="expand",
    )(a0, a1, b0, b1)


def cut_matrix(where, matrix, messages, local=()):
    width, parts, voxels = matrix.shape
    span = voxels // (XL * Z * CORE)
    piece = (width, parts, span)
    shapes = [(2, len(message)) + piece for message in messages] + [(len(steps),) + piece for steps, _ in local]
    count = 2 * sum(map(len, messages)) + sum(len(steps) for steps, _ in local)

    def kernel(place_ref, src, *rest):
        outs, sems = rest[:-1], rest[-1]
        xl, z, c = place_ref[2], place_ref[3], place_ref[4]
        wanted = [
            (s, 1, dc, out.at[dc, k]) for out, message in zip(outs, messages) for k, s in enumerate(message) for dc in range(2)
        ]
        for out, (steps, dc) in zip(outs[len(messages):], local):
            wanted += [(s, 0, dc, out.at[i]) for i, s in enumerate(steps)]
        copies = []
        for i, (s, dxl, dc, out) in enumerate(wanted):
            reader = (c + dc) % CORE
            at = (z + Z + (1 - 2 * reader) * TARGETS[s]) % Z
            first = (((xl + dxl) % XL * Z + at) * CORE + reader) * span
            columns = src.at[:, :, pl.ds(pl.multiple_of(first, span), span)]
            copies.append(pltpu.make_async_copy(columns, out, sems.at[i]))
        for copy in copies:
            copy.start()
        for copy in copies:
            copy.wait()

    return pl.pallas_call(
        kernel,
        in_specs=[SMEM, pl.BlockSpec(memory_space=pltpu.HBM)],
        out_specs=[VMEM] * len(shapes),
        out_shape=[jax.ShapeDtypeStruct(s, BF16) for s in shapes],
        scratch_shapes=[pltpu.SemaphoreType.DMA((count,))],
        compiler_params=PARAMS,
        cost_estimate=FREE,
        name="cut_matrix",
    )(where, pltpu.with_memory_space_constraint(matrix, pltpu.HBM))


def flatten_kernel(index, *refs):
    out = refs[-1]
    for n, (i, ref) in enumerate(zip(index, refs)):
        out[n] = ref[i].reshape(out.shape[1:])


def flatten(*pieces):
    arrays, index = zip(*pieces)
    width, parts, span = arrays[0].shape[-3:]
    return pl.pallas_call(
        functools.partial(flatten_kernel, index),
        out_shape=jax.ShapeDtypeStruct((4, width * parts, span), BF16),
        in_specs=[VMEM] * 4,
        out_specs=VMEM,
        compiler_params=PARAMS,
        cost_estimate=FREE,
        name="flatten",
    )(*arrays)


def term_kernel(el, ec, flat, *rest):
    dot = functools.partial(jnp.dot, preferred_element_type=F32)
    total = None if len(rest) == 1 else rest[0][...]
    for n, e in enumerate((el.at[0], ec.at[0], el.at[1], ec.at[1])):
        for h in range(2):
            d = dot(e[h], flat[n])
            total = d if total is None else total + d
    rest[-1][...] = total


def term(el, ec, flat, *so_far):
    return pl.pallas_call(
        term_kernel,
        out_shape=jax.ShapeDtypeStruct((el.shape[2], flat.shape[2]), F32),
        in_specs=[VMEM] * (3 + len(so_far)),
        out_specs=VMEM,
        compiler_params=PARAMS,
        cost_estimate=FREE,
        name="term",
    )(el, ec, flat, *so_far)


def finish_kernel(a, b, c, out):
    out[...] = (a[...] + b[...] + c[...]).reshape(out.shape)


def finish(*parts):
    rows, cols = parts[0].shape
    return pl.pallas_call(
        finish_kernel,
        out_shape=jax.ShapeDtypeStruct((rows // BR_DEV, BR_DEV, cols), F32),
        in_specs=[VMEM] * 3,
        out_specs=VMEM,
        compiler_params=PARAMS,
        cost_estimate=FREE,
        name="finish",
    )(*parts)


def on_device(residuals, system_matrix, offsets, patch_ids):
    xh, y, xl, z, c = place()
    where = jnp.stack([xh, y, xl, z, c]).astype(jnp.int32)
    rows, frames, parts, width = residuals.shape
    tc = frames * parts
    raw = residuals.reshape(rows, tc, width)
    pieces = [shift(raw, dy=-1), shift(raw, dy=2), shift(raw, dy=1)]
    (far,) = cut_matrix(where, system_matrix, MESSAGES[:1])
    fars = [across(far)]
    matrix, pieces[0] = lax.optimization_barrier((system_matrix, pieces[0]))
    early, late = MESSAGES[0], range(len(MESSAGES[0]), Z)
    *far, own, core = cut_matrix(where, matrix, MESSAGES[1:3], ((early, 0), (range(Z), 1)))
    sent = add_rows(where, offsets, patch_ids, [raw] + pieces)
    (same, plus, minus, other), fars[0], core = lax.optimization_barrier((sent, fars[0], core))
    rest = [shift(plus, dx=1), shift(minus, dx=-1), shift(other, dx=2)]
    core = shift(core, dc=1)
    cross = shift(fars[0][1], dc=1)
    flats = [flatten((own, (s,)), (core, (s,)), (fars[0], (0, s)), (cross, (s,))) for s in early]
    for i in range(2):
        far[i], rest[i] = lax.optimization_barrier((far[i], rest[i]))
        fars.append(across(far[i]))
    flats, rest = lax.optimization_barrier((flats, rest))
    from_left, from_right, across_two = rest
    el = expand(same, across_two, from_left, from_right)
    matrix, el = lax.optimization_barrier((matrix, el))
    ec = shift(el, dc=1)
    *more, own = cut_matrix(where, matrix, MESSAGES[3:], ((late, 0),))
    far += more
    fars.append(across(far[2]))

    sums = [None, None]
    for s in range(Z):
        if s >= 2:
            fars[s - 1], total = lax.optimization_barrier((fars[s - 1], total))
            sums[1 - s % 2] = shift(total, dz=2 * (s % 2) - 1, mirror=True)
            cross = shift(fars[s - 1][1], dc=1)
            flats.append(flatten((own, (s - 2,)), (core, (s,)), (fars[s - 1], (0, 0)), (cross, (0,))))
        if s == Z - 1:
            total = term(el, ec, flats[s])
            break
        total = term(el, ec, flats[s], *sums[s % 2:s % 2 + 1] if s > 1 else ())
        if s in PACE:
            ahead, total = lax.optimization_barrier((far[len(fars) - 1], total))
            fars.append(across(ahead))
        if s == 0:
            flats[1], total = lax.optimization_barrier((flats[1], total))
            sums[0] = shift(total, dz=1, mirror=True)
    volume = finish(total, *sums)
    return volume.reshape(frames, parts, BR_DEV, -1)


def across(far):
    return shift(far, dx=1, mirror=True)


def solution(mesh):
    in_specs = (P("grp", None, None, "freq"), P("freq", None, None), P(), P())
    out_specs = P(None, None, "grp", "freq")
    return jax.shard_map(
        on_device, mesh=mesh, in_specs=in_specs, out_specs=out_specs, check_vma=False
    )
```

```python
import functools

import jax
import jax.numpy as jnp
from jax import lax
from jax.experimental import pallas as pl
from jax.experimental.pallas import tpu as pltpu
from jax.sharding import PartitionSpec as P

XH, Y, XL, Z, CORE = 2, 4, 2, 8, 2
NX = XH * XL
BR_DEV = 4
TARGETS = (4, 3, -3, 2, -2, 1, -1, 0)
MESSAGES = ((0, 1), (2,), (3,), (4,), (5,), (6,), (7,))
PACE = (1, 2, 3)
FREE = pl.CostEstimate(flops=1000, bytes_accessed=1000, transcendentals=0)
PARAMS = pltpu.CompilerParams(vmem_limit_bytes=24 * 2**20)
SMEM = pl.BlockSpec(memory_space=pltpu.SMEM)
VMEM = pl.BlockSpec(memory_space=pltpu.VMEM)
F32, BF16 = jnp.float32, jnp.bfloat16


def linear(xh, y, xl, z, c):
    return (((xh * Y + y) * XL + xl) * Z + z) * CORE + c


def shift(array, dx=0, dy=0, dz=0, dc=0, mirror=False):
    pairs = []
    for x in range(NX):
        for y in range(Y):
            for z in range(Z):
                for c in range(CORE):
                    way = -1 if mirror and c else 1
                    tx = (x + way * dx) % NX
                    ty, tz, t = (y + way * dy) % Y, (z + way * dz) % Z, (c + dc) % CORE
                    pairs.append((linear(x // 2, y, x % 2, z, c), linear(tx // 2, ty, tx % 2, tz, t)))
    return lax.ppermute(array, ("grp", "freq"), pairs)


def place():
    grp, freq = lax.axis_index("grp"), lax.axis_index("freq")
    return grp >> 2, grp & 3, freq >> 4, (freq >> 1) & 7, freq & 1


def add_rows_kernel(place_ref, offs_ref, ids_ref, r0, r1, r2, r3, same, plus, minus, other, acc):
    xh, y, xl = place_ref[0], place_ref[1], place_ref[2]
    rows = r0.shape[0]
    acc[...] = jnp.zeros_like(acc)
    for dy, ref in enumerate((r0, r1, r2, r3)):
        first = (xh * Y + (y + dy) % Y) * rows
        for i in range(rows):
            brick = offs_ref[ids_ref[first + i]]
            owner = brick // BR_DEV
            slot = (owner // Y) * BR_DEV + brick % BR_DEV
            slot = jnp.where(owner % Y == y, slot, XH * BR_DEV)
            acc[slot] += ref[i].astype(F32)
    here, there = pl.ds(xh * BR_DEV, BR_DEV), pl.ds((1 - xh) * BR_DEV, BR_DEV)
    same[...] = acc[here]
    other[...] = acc[there]
    right = jnp.where(xl == 0, xh, 1 - xh)
    plus[...] = acc[pl.ds(right * BR_DEV, BR_DEV)]
    minus[...] = acc[pl.ds((1 - right) * BR_DEV, BR_DEV)]


def add_rows(where, offsets, patch_ids, pieces):
    tc, width = pieces[0].shape[1:]
    out = jax.ShapeDtypeStruct((BR_DEV, tc, width), F32)
    return pl.pallas_call(
        add_rows_kernel,
        out_shape=[out] * 4,
        in_specs=[SMEM] * 3 + [VMEM] * 4,
        out_specs=[VMEM] * 4,
        compiler_params=PARAMS,
        cost_estimate=FREE,
        scratch_shapes=[pltpu.VMEM((XH * BR_DEV + 1, tc, width), F32)],
        name="add_rows",
    )(where, offsets, patch_ids, *pieces)


def expand_kernel(a0, a1, b0, b1, out):
    bricks, tc, width = a0.shape
    rows, depth = bricks * tc, 2 * width
    r = lax.broadcasted_iota(jnp.int32, (rows, rows), 0)
    s = lax.broadcasted_iota(jnp.int32, (rows, rows), 1)
    reorder = (s == (r % bricks) * tc + r // bricks).astype(F32).astype(BF16)
    f = lax.broadcasted_iota(jnp.int32, (depth, depth), 0)
    k = lax.broadcasted_iota(jnp.int32, (depth, depth), 1)
    weave = (k == 2 * (f % width) + f // width).astype(F32).astype(BF16)
    part = lax.broadcasted_iota(jnp.int32, (rows, width), 0) % 2
    dot = functools.partial(jnp.dot, preferred_element_type=F32)
    parts = []
    for u, v in ((a0, a1), (b0, b1)):
        x = (u[...] + v[...]).reshape(rows, width)
        xs = jnp.where(part == 0, pltpu.roll(x, rows - 1, 0), -pltpu.roll(x, 1, 0))
        both = jnp.concatenate([x, xs], axis=1)
        hi = both.astype(BF16)
        parts += [hi, (both - hi.astype(F32)).astype(BF16)]
    woven = dot(jnp.concatenate(parts, axis=0), weave).astype(BF16)
    wide = jnp.concatenate([woven[i * rows:(i + 1) * rows] for i in range(4)], axis=1)
    wide = dot(reorder, wide).astype(BF16)
    for i in range(4):
        out[i // 2, i % 2] = wide[:, i * depth:(i + 1) * depth]


def expand(a0, a1, b0, b1):
    bricks, tc, width = a0.shape
    rows = bricks * tc
    return pl.pallas_call(
        expand_kernel,
        out_shape=jax.ShapeDtypeStruct((2, 2, rows, 2 * width), BF16),
        in_specs=[VMEM] * 4,
        out_specs=VMEM,
        compiler_params=PARAMS,
        cost_estimate=FREE,
        name="expand",
    )(a0, a1, b0, b1)


def cut_matrix(where, matrix, messages, local=()):
    width, parts, voxels = matrix.shape
    span = voxels // (XL * Z * CORE)
    piece = (width, parts, span)
    shapes = [(2, len(message)) + piece for message in messages] + [(len(steps),) + piece for steps, _ in local]
    count = 2 * sum(map(len, messages)) + sum(len(steps) for steps, _ in local)

    def kernel(place_ref, src, *rest):
        outs, sems = rest[:-1], rest[-1]
        xl, z, c = place_ref[2], place_ref[3], place_ref[4]
        wanted = [
            (s, 1, dc, out.at[dc, k]) for out, message in zip(outs, messages) for k, s in enumerate(message) for dc in range(2)
        ]
        for out, (steps, dc) in zip(outs[len(messages):], local):
            wanted += [(s, 0, dc, out.at[i]) for i, s in enumerate(steps)]
        copies = []
        for i, (s, dxl, dc, out) in enumerate(wanted):
            reader = (c + dc) % CORE
            at = (z + Z + (1 - 2 * reader) * TARGETS[s]) % Z
            first = (((xl + dxl) % XL * Z + at) * CORE + reader) * span
            columns = src.at[:, :, pl.ds(pl.multiple_of(first, span), span)]
            copies.append(pltpu.make_async_copy(columns, out, sems.at[i]))
        for copy in copies:
            copy.start()
        for copy in copies:
            copy.wait()

    return pl.pallas_call(
        kernel,
        in_specs=[SMEM, pl.BlockSpec(memory_space=pltpu.HBM)],
        out_specs=[VMEM] * len(shapes),
        out_shape=[jax.ShapeDtypeStruct(s, BF16) for s in shapes],
        scratch_shapes=[pltpu.SemaphoreType.DMA((count,))],
        compiler_params=PARAMS,
        cost_estimate=FREE,
        name="cut_matrix",
    )(where, pltpu.with_memory_space_constraint(matrix, pltpu.HBM))


def flatten_kernel(index, *refs):
    out = refs[-1]
    for n, (i, ref) in enumerate(zip(index, refs)):
        out[n] = ref[i].reshape(out.shape[1:])


def flatten(*pieces):
    arrays, index = zip(*pieces)
    width, parts, span = arrays[0].shape[-3:]
    return pl.pallas_call(
        functools.partial(flatten_kernel, index),
        out_shape=jax.ShapeDtypeStruct((4, width * parts, span), BF16),
        in_specs=[VMEM] * 4,
        out_specs=VMEM,
        compiler_params=PARAMS,
        cost_estimate=FREE,
        name="flatten",
    )(*arrays)


def term_kernel(at, el, ec, flat, *rest):
    dot = functools.partial(jnp.dot, preferred_element_type=F32)
    out = rest[-1]
    total = None
    for n, e in enumerate((el.at[0], ec.at[0], el.at[1], ec.at[1])):
        for h in range(2):
            d = dot(e[h], flat[n])
            total = d if total is None else total + d
    out[...] = total
    if len(rest) > 1:
        columns = pl.ds(at, rest[0].shape[1])
        out[:, columns] += rest[0][...]


def term(el, ec, flat, *so_far, at=0):
    return pl.pallas_call(
        functools.partial(term_kernel, at),
        out_shape=jax.ShapeDtypeStruct((el.shape[2], flat.shape[2]), F32),
        in_specs=[VMEM] * (3 + len(so_far)),
        out_specs=VMEM,
        compiler_params=PARAMS,
        cost_estimate=FREE,
        name="term",
    )(el, ec, flat, *so_far)


def finish_kernel(a, b, c, out):
    out[...] = (a[...] + b[...] + c[...]).reshape(out.shape)


def finish(*parts):
    rows, cols = parts[0].shape
    return pl.pallas_call(
        finish_kernel,
        out_shape=jax.ShapeDtypeStruct((rows // BR_DEV, BR_DEV, cols), F32),
        in_specs=[VMEM] * 3,
        out_specs=VMEM,
        compiler_params=PARAMS,
        cost_estimate=FREE,
        name="finish",
    )(*parts)


def on_device(residuals, system_matrix, offsets, patch_ids):
    xh, y, xl, z, c = place()
    where = jnp.stack([xh, y, xl, z, c]).astype(jnp.int32)
    rows, frames, parts, width = residuals.shape
    tc = frames * parts
    raw = residuals.reshape(rows, tc, width)
    pieces = [shift(raw, dy=-1), shift(raw, dy=2), shift(raw, dy=1)]
    (far,) = cut_matrix(where, system_matrix, MESSAGES[:1])
    fars = [across(far)]
    matrix, pieces[0] = lax.optimization_barrier((system_matrix, pieces[0]))
    early, late = MESSAGES[0], range(len(MESSAGES[0]), Z)
    *far, own, core = cut_matrix(where, matrix, MESSAGES[1:2], ((early, 0), (range(Z), 1)))
    sent = add_rows(where, offsets, patch_ids, [raw] + pieces)
    (same, plus, minus, other), fars[0], core = lax.optimization_barrier((sent, fars[0], core))
    rest = [shift(plus, dx=1), shift(minus, dx=-1), shift(other, dx=2)]
    core = shift(core, dc=1)
    cross = shift(fars[0][1], dc=1)
    flats = [flatten((own, (s,)), (core, (s,)), (fars[0], (0, s)), (cross, (s,))) for s in early]
    far[0], rest[0] = lax.optimization_barrier((far[0], rest[0]))
    fars.append(across(far[0]))
    flats, rest = lax.optimization_barrier((flats, rest))
    from_left, from_right, across_two = rest
    el = expand(same, across_two, from_left, from_right)
    matrix, el = lax.optimization_barrier((matrix, el))
    ec = shift(el, dc=1)
    *more, own = cut_matrix(where, matrix, MESSAGES[2:], ((late, 0),))
    far += more
    fars += [across(f) for f in far[1:3]]

    sums = [None, None]
    for s in range(Z):
        if s >= 2:
            fars[s - 1], total = lax.optimization_barrier((fars[s - 1], total))
            sums[s % 2] = shift(total, dz=1 - 2 * (s % 2), mirror=True)
            cross = shift(fars[s - 1][1], dc=1)
            flats.append(flatten((own, (s - 2,)), (core, (s,)), (fars[s - 1], (0, 0)), (cross, (0,))))
        if s in (0, Z - 1):
            total = term(el, ec, flats[s])
        else:
            total = term(el, ec, flats[s], sums[1 - s % 2], at=total.shape[1] // 2 if s == 2 else 0)
        if s in PACE:
            ahead, total = lax.optimization_barrier((far[len(fars) - 1], total))
            fars.append(across(ahead))
        if s == 0:
            flats[1], total = lax.optimization_barrier((flats[1], total))
            half = total.shape[1] // 2
            sums = [shift(total[:, :half], dz=1, mirror=True), shift(total[:, half:], dz=-1, mirror=True)]
    volume = finish(total, *sums)
    return volume.reshape(frames, parts, BR_DEV, -1)


def across(far):
    return shift(far, dx=1, mirror=True)


def solution(mesh):
    in_specs = (P("grp", None, None, "freq"), P("freq", None, None), P(), P())
    out_specs = P(None, None, "grp", "freq")
    return jax.shard_map(
        on_device, mesh=mesh, in_specs=in_specs, out_specs=out_specs, check_vma=False
    )
```

```python
import functools

import jax
import jax.numpy as jnp
from jax import lax
from jax.experimental import pallas as pl
from jax.experimental.pallas import tpu as pltpu
from jax.sharding import PartitionSpec as P

XH, Y, XL, Z, CORE = 2, 4, 2, 8, 2
NX = XH * XL
BR_DEV = 4
TARGETS = (4, -3, 3, -2, 2, -1, 1, 0)
MESSAGES = ((0, 1), (2,), (3,), (4,), (5,), (6,), (7,))
PACE = (1, 2, 3)
FREE = pl.CostEstimate(flops=1000, bytes_accessed=1000, transcendentals=0)
PARAMS = pltpu.CompilerParams(vmem_limit_bytes=24 * 2**20)
SMEM = pl.BlockSpec(memory_space=pltpu.SMEM)
VMEM = pl.BlockSpec(memory_space=pltpu.VMEM)
F32, BF16 = jnp.float32, jnp.bfloat16


def linear(xh, y, xl, z, c):
    return (((xh * Y + y) * XL + xl) * Z + z) * CORE + c


def shift(array, dx=0, dy=0, dz=0, dc=0, mirror=False):
    pairs = []
    for x in range(NX):
        for y in range(Y):
            for z in range(Z):
                for c in range(CORE):
                    way = -1 if mirror and c else 1
                    tx = (x + way * dx) % NX
                    ty, tz, t = (y + way * dy) % Y, (z + way * dz) % Z, (c + dc) % CORE
                    pairs.append((linear(x // 2, y, x % 2, z, c), linear(tx // 2, ty, tx % 2, tz, t)))
    return lax.ppermute(array, ("grp", "freq"), pairs)


def place():
    grp, freq = lax.axis_index("grp"), lax.axis_index("freq")
    return grp >> 2, grp & 3, freq >> 4, (freq >> 1) & 7, freq & 1


def add_rows_kernel(place_ref, offs_ref, ids_ref, r0, r1, r2, r3, same, plus, minus, other, acc):
    xh, y, xl = place_ref[0], place_ref[1], place_ref[2]
    rows = r0.shape[0]
    acc[...] = jnp.zeros_like(acc)
    for dy, ref in enumerate((r0, r1, r2, r3)):
        first = (xh * Y + (y + dy) % Y) * rows
        for i in range(rows):
            brick = offs_ref[ids_ref[first + i]]
            owner = brick // BR_DEV
            slot = (owner // Y) * BR_DEV + brick % BR_DEV
            slot = jnp.where(owner % Y == y, slot, XH * BR_DEV)
            acc[slot] += ref[i].astype(F32)
    here, there = pl.ds(xh * BR_DEV, BR_DEV), pl.ds((1 - xh) * BR_DEV, BR_DEV)
    same[...] = acc[here]
    other[...] = acc[there]
    right = jnp.where(xl == 0, xh, 1 - xh)
    plus[...] = acc[pl.ds(right * BR_DEV, BR_DEV)]
    minus[...] = acc[pl.ds((1 - right) * BR_DEV, BR_DEV)]


def add_rows(where, offsets, patch_ids, pieces):
    tc, width = pieces[0].shape[1:]
    out = jax.ShapeDtypeStruct((BR_DEV, tc, width), F32)
    return pl.pallas_call(
        add_rows_kernel,
        out_shape=[out] * 4,
        in_specs=[SMEM] * 3 + [VMEM] * 4,
        out_specs=[VMEM] * 4,
        compiler_params=PARAMS,
        cost_estimate=FREE,
        scratch_shapes=[pltpu.VMEM((XH * BR_DEV + 1, tc, width), F32)],
        name="add_rows",
    )(where, offsets, patch_ids, *pieces)


def expand_kernel(a0, a1, b0, b1, out):
    bricks, tc, width = a0.shape
    rows, depth = bricks * tc, 2 * width
    r = lax.broadcasted_iota(jnp.int32, (rows, rows), 0)
    s = lax.broadcasted_iota(jnp.int32, (rows, rows), 1)
    reorder = (s == (r % bricks) * tc + r // bricks).astype(F32).astype(BF16)
    f = lax.broadcasted_iota(jnp.int32, (depth, depth), 0)
    k = lax.broadcasted_iota(jnp.int32, (depth, depth), 1)
    weave = (k == 2 * (f % width) + f // width).astype(F32).astype(BF16)
    part = lax.broadcasted_iota(jnp.int32, (rows, width), 0) % 2
    dot = functools.partial(jnp.dot, preferred_element_type=F32)
    parts = []
    for u, v in ((a0, a1), (b0, b1)):
        x = (u[...] + v[...]).reshape(rows, width)
        xs = jnp.where(part == 0, pltpu.roll(x, rows - 1, 0), -pltpu.roll(x, 1, 0))
        both = jnp.concatenate([x, xs], axis=1)
        hi = both.astype(BF16)
        parts += [hi, (both - hi.astype(F32)).astype(BF16)]
    woven = dot(jnp.concatenate(parts, axis=0), weave).astype(BF16)
    wide = jnp.concatenate([woven[i * rows:(i + 1) * rows] for i in range(4)], axis=1)
    wide = dot(reorder, wide).astype(BF16)
    for i in range(4):
        out[i // 2, i % 2] = wide[:, i * depth:(i + 1) * depth]


def expand(a0, a1, b0, b1):
    bricks, tc, width = a0.shape
    rows = bricks * tc
    return pl.pallas_call(
        expand_kernel,
        out_shape=jax.ShapeDtypeStruct((2, 2, rows, 2 * width), BF16),
        in_specs=[VMEM] * 4,
        out_specs=VMEM,
        compiler_params=PARAMS,
        cost_estimate=FREE,
        name="expand",
    )(a0, a1, b0, b1)


def cut_matrix(where, matrix, messages, local=()):
    width, parts, voxels = matrix.shape
    span = voxels // (XL * Z * CORE)
    piece = (width, parts, span)
    shapes = [(2, len(message)) + piece for message in messages] + [(len(steps),) + piece for steps, _ in local]
    count = 2 * sum(map(len, messages)) + sum(len(steps) for steps, _ in local)

    def kernel(place_ref, src, *rest):
        outs, sems = rest[:-1], rest[-1]
        xl, z, c = place_ref[2], place_ref[3], place_ref[4]
        wanted = [
            (s, 1, dc, out.at[dc, k]) for out, message in zip(outs, messages) for k, s in enumerate(message) for dc in range(2)
        ]
        for out, (steps, dc) in zip(outs[len(messages):], local):
            wanted += [(s, 0, dc, out.at[i]) for i, s in enumerate(steps)]
        copies = []
        for i, (s, dxl, dc, out) in enumerate(wanted):
            reader = (c + dc) % CORE
            at = (z + Z + (1 - 2 * reader) * TARGETS[s]) % Z
            first = (((xl + dxl) % XL * Z + at) * CORE + reader) * span
            columns = src.at[:, :, pl.ds(pl.multiple_of(first, span), span)]
            copies.append(pltpu.make_async_copy(columns, out, sems.at[i]))
        for copy in copies:
            copy.start()
        for copy in copies:
            copy.wait()

    return pl.pallas_call(
        kernel,
        in_specs=[SMEM, pl.BlockSpec(memory_space=pltpu.HBM)],
        out_specs=[VMEM] * len(shapes),
        out_shape=[jax.ShapeDtypeStruct(s, BF16) for s in shapes],
        scratch_shapes=[pltpu.SemaphoreType.DMA((count,))],
        compiler_params=PARAMS,
        cost_estimate=FREE,
        name="cut_matrix",
    )(where, pltpu.with_memory_space_constraint(matrix, pltpu.HBM))


def flatten_kernel(index, *refs):
    out = refs[-1]
    for n, (i, ref) in enumerate(zip(index, refs)):
        out[n] = ref[i].reshape(out.shape[1:])


def flatten(*pieces):
    arrays, index = zip(*pieces)
    width, parts, span = arrays[0].shape[-3:]
    return pl.pallas_call(
        functools.partial(flatten_kernel, index),
        out_shape=jax.ShapeDtypeStruct((4, width * parts, span), BF16),
        in_specs=[VMEM] * 4,
        out_specs=VMEM,
        compiler_params=PARAMS,
        cost_estimate=FREE,
        name="flatten",
    )(*arrays)


def term_kernel(el, ec, flat, *rest):
    dot = functools.partial(jnp.dot, preferred_element_type=F32)
    total = None if len(rest) == 1 else rest[0][...]
    for n, e in enumerate((el.at[0], ec.at[0], el.at[1], ec.at[1])):
        for h in range(2):
            d = dot(e[h], flat[n])
            total = d if total is None else total + d
    rest[-1][...] = total


def term(el, ec, flat, *so_far):
    return pl.pallas_call(
        term_kernel,
        out_shape=jax.ShapeDtypeStruct((el.shape[2], flat.shape[2]), F32),
        in_specs=[VMEM] * (3 + len(so_far)),
        out_specs=VMEM,
        compiler_params=PARAMS,
        cost_estimate=FREE,
        name="term",
    )(el, ec, flat, *so_far)


def finish_kernel(a, b, c, out):
    out[...] = (a[...] + b[...] + c[...]).reshape(out.shape)


def finish(*parts):
    rows, cols = parts[0].shape
    return pl.pallas_call(
        finish_kernel,
        out_shape=jax.ShapeDtypeStruct((rows // BR_DEV, BR_DEV, cols), F32),
        in_specs=[VMEM] * 3,
        out_specs=VMEM,
        compiler_params=PARAMS,
        cost_estimate=FREE,
        name="finish",
    )(*parts)


def on_device(residuals, system_matrix, offsets, patch_ids):
    xh, y, xl, z, c = place()
    where = jnp.stack([xh, y, xl, z, c]).astype(jnp.int32)
    rows, frames, parts, width = residuals.shape
    tc = frames * parts
    raw = residuals.reshape(rows, tc, width)
    pieces = [shift(raw, dy=-1), shift(raw, dy=2), shift(raw, dy=1)]
    (far,) = cut_matrix(where, system_matrix, MESSAGES[:1])
    fars = [across(far)]
    matrix, pieces[0] = lax.optimization_barrier((system_matrix, pieces[0]))
    early, late = MESSAGES[0], range(len(MESSAGES[0]), Z)
    *far, own, core = cut_matrix(where, matrix, MESSAGES[1:2], ((early, 0), (range(Z), 1)))
    sent = add_rows(where, offsets, patch_ids, [raw] + pieces)
    (same, plus, minus, other), fars[0], core = lax.optimization_barrier((sent, fars[0], core))
    rest = [shift(plus, dx=1), shift(minus, dx=-1), shift(other, dx=2)]
    core = shift(core, dc=1)
    cross = shift(fars[0][1], dc=1)
    flats = [flatten((own, (s,)), (core, (s,)), (fars[0], (0, s)), (cross, (s,))) for s in early]
    far[0], rest[0] = lax.optimization_barrier((far[0], rest[0]))
    fars.append(across(far[0]))
    flats, rest = lax.optimization_barrier((flats, rest))
    from_left, from_right, across_two = rest
    el = expand(same, across_two, from_left, from_right)
    matrix, el = lax.optimization_barrier((matrix, el))
    ec = shift(el, dc=1)
    *more, own = cut_matrix(where, matrix, MESSAGES[2:], ((late, 0),))
    far += more
    fars += [across(f) for f in far[1:3]]

    sums = [None, None]
    for s in range(Z):
        if s >= 2:
            fars[s - 1], total = lax.optimization_barrier((fars[s - 1], total))
            sums[1 - s % 2] = shift(total, dz=2 * (s % 2) - 1, mirror=True)
            cross = shift(fars[s - 1][1], dc=1)
            flats.append(flatten((own, (s - 2,)), (core, (s,)), (fars[s - 1], (0, 0)), (cross, (0,))))
        if s == Z - 1:
            total = term(el, ec, flats[s])
            break
        total = term(el, ec, flats[s])
        if s > 1:
            total = sums[s % 2] + total
        if s in PACE:
            ahead, total = lax.optimization_barrier((far[len(fars) - 1], total))
            fars.append(across(ahead))
        if s == 0:
            flats[1], total = lax.optimization_barrier((flats[1], total))
            sums[0] = shift(total, dz=1, mirror=True)
    volume = finish(total, *sums)
    return volume.reshape(frames, parts, BR_DEV, -1)


def across(far):
    return shift(far, dx=1, mirror=True)


def solution(mesh):
    in_specs = (P("grp", None, None, "freq"), P("freq", None, None), P(), P())
    out_specs = P(None, None, "grp", "freq")
    return jax.shard_map(
        on_device, mesh=mesh, in_specs=in_specs, out_specs=out_specs, check_vma=False
    )
```

```python
import functools

import jax
import jax.numpy as jnp
from jax import lax
from jax.experimental import pallas as pl
from jax.experimental.pallas import tpu as pltpu
from jax.sharding import PartitionSpec as P

XH, Y, XL, Z, CORE = 2, 4, 2, 8, 2
NX = XH * XL
BR_DEV = 4
TARGETS = (4, -3, 3, -2, 2, -1, 1, 0)
MESSAGES = ((0, 1), (2,), (3,), (4,), (5,), (6,), (7,))
PACE = (1, 2, 3)
FREE = pl.CostEstimate(flops=1000, bytes_accessed=1000, transcendentals=0)
PARAMS = pltpu.CompilerParams(vmem_limit_bytes=24 * 2**20)
SMEM = pl.BlockSpec(memory_space=pltpu.SMEM)
VMEM = pl.BlockSpec(memory_space=pltpu.VMEM)
F32, BF16 = jnp.float32, jnp.bfloat16


def linear(xh, y, xl, z, c):
    return (((xh * Y + y) * XL + xl) * Z + z) * CORE + c


def shift(array, dx=0, dy=0, dz=0, dc=0, mirror=False):
    pairs = []
    for x in range(NX):
        for y in range(Y):
            for z in range(Z):
                for c in range(CORE):
                    way = -1 if mirror and c else 1
                    tx = (x + way * dx) % NX
                    ty, tz, t = (y + way * dy) % Y, (z + way * dz) % Z, (c + dc) % CORE
                    pairs.append((linear(x // 2, y, x % 2, z, c), linear(tx // 2, ty, tx % 2, tz, t)))
    return lax.ppermute(array, ("grp", "freq"), pairs)


def place():
    grp, freq = lax.axis_index("grp"), lax.axis_index("freq")
    return grp >> 2, grp & 3, freq >> 4, (freq >> 1) & 7, freq & 1


def add_rows_kernel(place_ref, offs_ref, ids_ref, r0, r1, r2, r3, same, plus, minus, other, acc):
    xh, y, xl = place_ref[0], place_ref[1], place_ref[2]
    rows = r0.shape[0]
    acc[...] = jnp.zeros_like(acc)
    for dy, ref in enumerate((r0, r1, r2, r3)):
        first = (xh * Y + (y + dy) % Y) * rows
        for i in range(rows):
            brick = offs_ref[ids_ref[first + i]]
            owner = brick // BR_DEV
            slot = (owner // Y) * BR_DEV + brick % BR_DEV
            slot = jnp.where(owner % Y == y, slot, XH * BR_DEV)
            acc[slot] += ref[i].astype(F32)
    here, there = pl.ds(xh * BR_DEV, BR_DEV), pl.ds((1 - xh) * BR_DEV, BR_DEV)
    same[...] = acc[here]
    other[...] = acc[there]
    right = jnp.where(xl == 0, xh, 1 - xh)
    plus[...] = acc[pl.ds(right * BR_DEV, BR_DEV)]
    minus[...] = acc[pl.ds((1 - right) * BR_DEV, BR_DEV)]


def add_rows(where, offsets, patch_ids, pieces):
    tc, width = pieces[0].shape[1:]
    out = jax.ShapeDtypeStruct((BR_DEV, tc, width), F32)
    return pl.pallas_call(
        add_rows_kernel,
        out_shape=[out] * 4,
        in_specs=[SMEM] * 3 + [VMEM] * 4,
        out_specs=[VMEM] * 4,
        compiler_params=PARAMS,
        cost_estimate=FREE,
        scratch_shapes=[pltpu.VMEM((XH * BR_DEV + 1, tc, width), F32)],
        name="add_rows",
    )(where, offsets, patch_ids, *pieces)


def sum_kernel(a0, a1, b0, b1, out):
    out[0] = a0[...] + a1[...]
    out[1] = b0[...] + b1[...]


def sum_rows(a0, a1, b0, b1):
    return pl.pallas_call(
        sum_kernel,
        out_shape=jax.ShapeDtypeStruct((2,) + a0.shape, F32),
        in_specs=[VMEM] * 4,
        out_specs=VMEM,
        compiler_params=PARAMS,
        cost_estimate=FREE,
        name="sum_rows",
    )(a0, a1, b0, b1)


def expand_kernel(here, there, out):
    bricks, tc, width = here.shape[1:]
    rows, depth = bricks * tc, 2 * width
    r = lax.broadcasted_iota(jnp.int32, (rows, rows), 0)
    s = lax.broadcasted_iota(jnp.int32, (rows, rows), 1)
    reorder = (s == (r % bricks) * tc + r // bricks).astype(F32).astype(BF16)
    f = lax.broadcasted_iota(jnp.int32, (depth, depth), 0)
    k = lax.broadcasted_iota(jnp.int32, (depth, depth), 1)
    weave = (k == 2 * (f % width) + f // width).astype(F32).astype(BF16)
    part = lax.broadcasted_iota(jnp.int32, (rows, width), 0) % 2
    dot = functools.partial(jnp.dot, preferred_element_type=F32)
    parts = []
    for source in (here.at[0], there.at[0], here.at[1], there.at[1]):
        x = source[...].reshape(rows, width)
        xs = jnp.where(part == 0, pltpu.roll(x, rows - 1, 0), -pltpu.roll(x, 1, 0))
        both = jnp.concatenate([x, xs], axis=1)
        hi = both.astype(BF16)
        parts += [hi, (both - hi.astype(F32)).astype(BF16)]
    woven = dot(jnp.concatenate(parts, axis=0), weave).astype(BF16)
    wide = jnp.concatenate([woven[i * rows:(i + 1) * rows] for i in range(8)], axis=1)
    wide = dot(reorder, wide).astype(BF16)
    for i in range(8):
        out[i // 2, i % 2] = wide[:, i * depth:(i + 1) * depth]


def expand(here, there):
    bricks, tc, width = here.shape[1:]
    rows = bricks * tc
    return pl.pallas_call(
        expand_kernel,
        out_shape=jax.ShapeDtypeStruct((4, 2, rows, 2 * width), BF16),
        in_specs=[VMEM] * 2,
        out_specs=VMEM,
        compiler_params=PARAMS,
        cost_estimate=FREE,
        name="expand",
    )(here, there)


def cut_matrix(where, matrix, messages, local=()):
    width, parts, voxels = matrix.shape
    span = voxels // (XL * Z * CORE)
    piece = (width, parts, span)
    shapes = [(2, len(message)) + piece for message in messages] + [(len(steps),) + piece for steps, _ in local]
    count = 2 * sum(map(len, messages)) + sum(len(steps) for steps, _ in local)

    def kernel(place_ref, src, *rest):
        outs, sems = rest[:-1], rest[-1]
        xl, z, c = place_ref[2], place_ref[3], place_ref[4]
        wanted = [
            (s, 1, dc, out.at[dc, k]) for out, message in zip(outs, messages) for k, s in enumerate(message) for dc in range(2)
        ]
        for out, (steps, dc) in zip(outs[len(messages):], local):
            wanted += [(s, 0, dc, out.at[i]) for i, s in enumerate(steps)]
        copies = []
        for i, (s, dxl, dc, out) in enumerate(wanted):
            reader = (c + dc) % CORE
            at = (z + Z + (1 - 2 * reader) * TARGETS[s]) % Z
            first = (((xl + dxl) % XL * Z + at) * CORE + reader) * span
            columns = src.at[:, :, pl.ds(pl.multiple_of(first, span), span)]
            copies.append(pltpu.make_async_copy(columns, out, sems.at[i]))
        for copy in copies:
            copy.start()
        for copy in copies:
            copy.wait()

    return pl.pallas_call(
        kernel,
        in_specs=[SMEM, pl.BlockSpec(memory_space=pltpu.HBM)],
        out_specs=[VMEM] * len(shapes),
        out_shape=[jax.ShapeDtypeStruct(s, BF16) for s in shapes],
        scratch_shapes=[pltpu.SemaphoreType.DMA((count,))],
        compiler_params=PARAMS,
        cost_estimate=FREE,
        name="cut_matrix",
    )(where, pltpu.with_memory_space_constraint(matrix, pltpu.HBM))


def flatten_kernel(index, *refs):
    out = refs[-1]
    for n, (i, ref) in enumerate(zip(index, refs)):
        out[n] = ref[i].reshape(out.shape[1:])


def flatten(*pieces):
    arrays, index = zip(*pieces)
    width, parts, span = arrays[0].shape[-3:]
    return pl.pallas_call(
        functools.partial(flatten_kernel, index),
        out_shape=jax.ShapeDtypeStruct((4, width * parts, span), BF16),
        in_specs=[VMEM] * 4,
        out_specs=VMEM,
        compiler_params=PARAMS,
        cost_estimate=FREE,
        name="flatten",
    )(*arrays)


def term_kernel(rows, flat, *rest):
    dot = functools.partial(jnp.dot, preferred_element_type=F32)
    total = None if len(rest) == 1 else rest[0][...]
    for n in range(4):
        for h in range(2):
            d = dot(rows[n, h], flat[n])
            total = d if total is None else total + d
    rest[-1][...] = total


def term(rows, flat, *so_far):
    return pl.pallas_call(
        term_kernel,
        out_shape=jax.ShapeDtypeStruct((rows.shape[2], flat.shape[2]), F32),
        in_specs=[VMEM] * (2 + len(so_far)),
        out_specs=VMEM,
        compiler_params=PARAMS,
        cost_estimate=FREE,
        name="term",
    )(rows, flat, *so_far)


def finish_kernel(a, b, c, out):
    out[...] = (a[...] + b[...] + c[...]).reshape(out.shape)


def finish(*parts):
    rows, cols = parts[0].shape
    return pl.pallas_call(
        finish_kernel,
        out_shape=jax.ShapeDtypeStruct((rows // BR_DEV, BR_DEV, cols), F32),
        in_specs=[VMEM] * 3,
        out_specs=VMEM,
        compiler_params=PARAMS,
        cost_estimate=FREE,
        name="finish",
    )(*parts)


def on_device(residuals, system_matrix, offsets, patch_ids):
    xh, y, xl, z, c = place()
    where = jnp.stack([xh, y, xl, z, c]).astype(jnp.int32)
    rows, frames, parts, width = residuals.shape
    tc = frames * parts
    raw = residuals.reshape(rows, tc, width)
    pieces = [shift(raw, dy=-1), shift(raw, dy=2), shift(raw, dy=1)]
    (far,) = cut_matrix(where, system_matrix, MESSAGES[:1])
    fars = [across(far)]
    matrix, pieces[0] = lax.optimization_barrier((system_matrix, pieces[0]))
    early, late = MESSAGES[0], range(len(MESSAGES[0]), Z)
    *far, own, core = cut_matrix(where, matrix, MESSAGES[1:3], ((early, 0), (range(Z), 1)))
    sent = add_rows(where, offsets, patch_ids, [raw] + pieces)
    (same, plus, minus, other), fars[0], core = lax.optimization_barrier((sent, fars[0], core))
    rest = [shift(plus, dx=1), shift(minus, dx=-1), shift(other, dx=2)]
    core = shift(core, dc=1)
    cross = shift(fars[0][1], dc=1)
    flats = [flatten((own, (s,)), (core, (s,)), (fars[0], (0, s)), (cross, (s,))) for s in early]
    far[:2], rest = lax.optimization_barrier((far[:2], rest))
    fars += [across(far[0]), across(far[1])]
    flats, rest = lax.optimization_barrier((flats, rest))
    from_left, from_right, across_two = rest
    here = sum_rows(same, across_two, from_left, from_right)
    matrix, here = lax.optimization_barrier((matrix, here))
    rows = expand(here, shift(here, dc=1))
    *more, own = cut_matrix(where, matrix, MESSAGES[3:], ((late, 0),))
    far += more
    fars.append(across(far[2]))

    sums = [None, None]
    for s in range(Z):
        if s >= 2:
            fars[s - 1], total = lax.optimization_barrier((fars[s - 1], total))
            sums[1 - s % 2] = shift(total, dz=2 * (s % 2) - 1, mirror=True)
            cross = shift(fars[s - 1][1], dc=1)
            flats.append(flatten((own, (s - 2,)), (core, (s,)), (fars[s - 1], (0, 0)), (cross, (0,))))
        if s == Z - 1:
            total = term(rows, flats[s])
            break
        total = term(rows, flats[s], *sums[s % 2:s % 2 + 1] if s > 1 else ())
        if s in PACE:
            ahead, total = lax.optimization_barrier((far[len(fars) - 1], total))
            fars.append(across(ahead))
        if s == 0:
            flats[1], total = lax.optimization_barrier((flats[1], total))
            sums[0] = shift(total, dz=1, mirror=True)
    volume = finish(total, *sums)
    return volume.reshape(frames, parts, BR_DEV, -1)


def across(far):
    return shift(far, dx=1, mirror=True)


def solution(mesh):
    in_specs = (P("grp", None, None, "freq"), P("freq", None, None), P(), P())
    out_specs = P(None, None, "grp", "freq")
    return jax.shard_map(
        on_device, mesh=mesh, in_specs=in_specs, out_specs=out_specs, check_vma=False
    )
```

```python
import functools

import jax
import jax.numpy as jnp
from jax import lax
from jax.experimental import pallas as pl
from jax.experimental.pallas import tpu as pltpu
from jax.sharding import PartitionSpec as P

XH, Y, XL, Z, CORE = 2, 4, 2, 8, 2
NX = XH * XL
BR_DEV = 4
TARGETS = (4, -3, 3, -2, 2, -1, 1, 0)
MESSAGES = ((0, 1), (2,), (3,), (4,), (5,), (6,), (7,))
PACE = (1, 2, 3)
FREE = pl.CostEstimate(flops=1000, bytes_accessed=1000, transcendentals=0)
PARAMS = pltpu.CompilerParams(vmem_limit_bytes=24 * 2**20)
SMEM = pl.BlockSpec(memory_space=pltpu.SMEM)
VMEM = pl.BlockSpec(memory_space=pltpu.VMEM)
F32, BF16 = jnp.float32, jnp.bfloat16


def linear(xh, y, xl, z, c):
    return (((xh * Y + y) * XL + xl) * Z + z) * CORE + c


def shift(array, dx=0, dy=0, dz=0, dc=0, mirror=False):
    pairs = []
    for x in range(NX):
        for y in range(Y):
            for z in range(Z):
                for c in range(CORE):
                    way = -1 if mirror and c else 1
                    tx = (x + way * dx) % NX
                    ty, tz, t = (y + way * dy) % Y, (z + way * dz) % Z, (c + dc) % CORE
                    pairs.append((linear(x // 2, y, x % 2, z, c), linear(tx // 2, ty, tx % 2, tz, t)))
    return lax.ppermute(array, ("grp", "freq"), pairs)


def place():
    grp, freq = lax.axis_index("grp"), lax.axis_index("freq")
    return grp >> 2, grp & 3, freq >> 4, (freq >> 1) & 7, freq & 1


def add_rows_kernel(place_ref, offs_ref, ids_ref, r0, r1, r2, r3, same, plus, minus, other, acc):
    xh, y, xl = place_ref[0], place_ref[1], place_ref[2]
    rows = r0.shape[0]
    acc[...] = jnp.zeros_like(acc)
    for dy, ref in enumerate((r0, r1, r2, r3)):
        first = (xh * Y + (y + dy) % Y) * rows
        for i in range(rows):
            brick = offs_ref[ids_ref[first + i]]
            owner = brick // BR_DEV
            slot = (owner // Y) * BR_DEV + brick % BR_DEV
            slot = jnp.where(owner % Y == y, slot, XH * BR_DEV)
            acc[slot] += ref[i].astype(F32)
    here, there = pl.ds(xh * BR_DEV, BR_DEV), pl.ds((1 - xh) * BR_DEV, BR_DEV)
    same[...] = acc[here]
    other[...] = acc[there]
    right = jnp.where(xl == 0, xh, 1 - xh)
    plus[...] = acc[pl.ds(right * BR_DEV, BR_DEV)]
    minus[...] = acc[pl.ds((1 - right) * BR_DEV, BR_DEV)]


def add_rows(where, offsets, patch_ids, pieces):
    tc, width = pieces[0].shape[1:]
    out = jax.ShapeDtypeStruct((BR_DEV, tc, width), F32)
    return pl.pallas_call(
        add_rows_kernel,
        out_shape=[out] * 4,
        in_specs=[SMEM] * 3 + [VMEM] * 4,
        out_specs=[VMEM] * 4,
        compiler_params=PARAMS,
        cost_estimate=FREE,
        scratch_shapes=[pltpu.VMEM((XH * BR_DEV + 1, tc, width), F32)],
        name="add_rows",
    )(where, offsets, patch_ids, *pieces)


def expand_kernel(a0, a1, b0, b1, out):
    bricks, tc, width = a0.shape
    rows, depth = bricks * tc, 2 * width
    r = lax.broadcasted_iota(jnp.int32, (rows, rows), 0)
    s = lax.broadcasted_iota(jnp.int32, (rows, rows), 1)
    reorder = (s == (r % bricks) * tc + r // bricks).astype(F32).astype(BF16)
    f = lax.broadcasted_iota(jnp.int32, (depth, depth), 0)
    k = lax.broadcasted_iota(jnp.int32, (depth, depth), 1)
    weave = (k == 2 * (f % width) + f // width).astype(F32).astype(BF16)
    part = lax.broadcasted_iota(jnp.int32, (rows, width), 0) % 2
    dot = functools.partial(jnp.dot, preferred_element_type=F32)
    parts = []
    for u, v in ((a0, a1), (b0, b1)):
        x = (u[...] + v[...]).reshape(rows, width)
        xs = jnp.where(part == 0, pltpu.roll(x, rows - 1, 0), -pltpu.roll(x, 1, 0))
        both = jnp.concatenate([x, xs], axis=1)
        hi = both.astype(BF16)
        parts += [hi, (both - hi.astype(F32)).astype(BF16)]
    woven = dot(jnp.concatenate(parts, axis=0), weave).astype(BF16)
    wide = jnp.concatenate([woven[i * rows:(i + 1) * rows] for i in range(4)], axis=1)
    wide = dot(reorder, wide).astype(BF16)
    for i in range(4):
        out[i // 2, i % 2] = wide[:, i * depth:(i + 1) * depth]


def expand(a0, a1, b0, b1):
    bricks, tc, width = a0.shape
    rows = bricks * tc
    return pl.pallas_call(
        expand_kernel,
        out_shape=jax.ShapeDtypeStruct((2, 2, rows, 2 * width), BF16),
        in_specs=[VMEM] * 4,
        out_specs=VMEM,
        compiler_params=PARAMS,
        cost_estimate=FREE,
        name="expand",
    )(a0, a1, b0, b1)


def cut_matrix(where, matrix, messages, local=()):
    width, parts, voxels = matrix.shape
    span = voxels // (XL * Z * CORE)
    piece = (width, parts, span)
    shapes = [(2, len(message)) + piece for message in messages] + [(len(steps),) + piece for steps, _ in local]
    count = 2 * sum(map(len, messages)) + sum(len(steps) for steps, _ in local)

    def kernel(place_ref, src, *rest):
        outs, sems = rest[:-1], rest[-1]
        xl, z, c = place_ref[2], place_ref[3], place_ref[4]
        wanted = [
            (s, 1, dc, out.at[dc, k]) for out, message in zip(outs, messages) for k, s in enumerate(message) for dc in range(2)
        ]
        for out, (steps, dc) in zip(outs[len(messages):], local):
            wanted += [(s, 0, dc, out.at[i]) for i, s in enumerate(steps)]
        copies = []
        for i, (s, dxl, dc, out) in enumerate(wanted):
            reader = (c + dc) % CORE
            at = (z + Z + (1 - 2 * reader) * TARGETS[s]) % Z
            first = (((xl + dxl) % XL * Z + at) * CORE + reader) * span
            columns = src.at[:, :, pl.ds(pl.multiple_of(first, span), span)]
            copies.append(pltpu.make_async_copy(columns, out, sems.at[i]))
        for copy in copies:
            copy.start()
        for copy in copies:
            copy.wait()

    return pl.pallas_call(
        kernel,
        in_specs=[SMEM, pl.BlockSpec(memory_space=pltpu.HBM)],
        out_specs=[VMEM] * len(shapes),
        out_shape=[jax.ShapeDtypeStruct(s, BF16) for s in shapes],
        scratch_shapes=[pltpu.SemaphoreType.DMA((count,))],
        compiler_params=PARAMS,
        cost_estimate=FREE,
        name="cut_matrix",
    )(where, pltpu.with_memory_space_constraint(matrix, pltpu.HBM))


def flatten_kernel(index, *refs):
    out = refs[-1]
    for n, (i, ref) in enumerate(zip(index, refs)):
        out[n] = ref[i].reshape(out.shape[1:])


def flatten(*pieces):
    arrays, index = zip(*pieces)
    width, parts, span = arrays[0].shape[-3:]
    return pl.pallas_call(
        functools.partial(flatten_kernel, index),
        out_shape=jax.ShapeDtypeStruct((4, width * parts, span), BF16),
        in_specs=[VMEM] * 4,
        out_specs=VMEM,
        compiler_params=PARAMS,
        cost_estimate=FREE,
        name="flatten",
    )(*arrays)


def term_kernel(el, ec, flat, *rest):
    dot = functools.partial(jnp.dot, preferred_element_type=F32)
    total = None if len(rest) == 1 else rest[0][...]
    for n, e in enumerate((el.at[0], ec.at[0], el.at[1], ec.at[1])):
        for h in range(2):
            d = dot(e[h], flat[n])
            total = d if total is None else total + d
    rest[-1][...] = total


def term(el, ec, flat, *so_far):
    return pl.pallas_call(
        term_kernel,
        out_shape=jax.ShapeDtypeStruct((el.shape[2], flat.shape[2]), F32),
        in_specs=[VMEM] * (3 + len(so_far)),
        out_specs=VMEM,
        compiler_params=PARAMS,
        cost_estimate=FREE,
        name="term",
    )(el, ec, flat, *so_far)


def finish_kernel(a, b, c, out):
    out[...] = (a[...] + b[...] + c[...]).reshape(out.shape)


def finish(*parts):
    rows, cols = parts[0].shape
    return pl.pallas_call(
        finish_kernel,
        out_shape=jax.ShapeDtypeStruct((rows // BR_DEV, BR_DEV, cols), F32),
        in_specs=[VMEM] * 3,
        out_specs=VMEM,
        compiler_params=PARAMS,
        cost_estimate=FREE,
        name="finish",
    )(*parts)


def on_device(residuals, system_matrix, offsets, patch_ids):
    xh, y, xl, z, c = place()
    where = jnp.stack([xh, y, xl, z, c]).astype(jnp.int32)
    rows, frames, parts, width = residuals.shape
    tc = frames * parts
    raw = residuals.reshape(rows, tc, width)
    pieces = [shift(raw, dy=-1), shift(raw, dy=2), shift(raw, dy=1)]
    (far,) = cut_matrix(where, system_matrix, MESSAGES[:1])
    fars = [across(far)]
    matrix, pieces[0] = lax.optimization_barrier((system_matrix, pieces[0]))
    early, late = MESSAGES[0], range(len(MESSAGES[0]), Z)
    *far, own, core = cut_matrix(where, matrix, MESSAGES[1:2], ((early, 0), (range(Z), 1)))
    sent = add_rows(where, offsets, patch_ids, [raw] + pieces)
    (same, plus, minus, other), fars[0], core = lax.optimization_barrier((sent, fars[0], core))
    rest = [shift(plus, dx=1), shift(minus, dx=-1), shift(other, dx=2)]
    core = shift(core, dc=1)
    cross = shift(fars[0][1], dc=1)
    flats = [flatten((own, (s,)), (core, (s,)), (fars[0], (0, s)), (cross, (s,))) for s in early]
    far[0], rest[2] = lax.optimization_barrier((far[0], rest[2]))
    fars.append(across(far[0]))
    flats, rest = lax.optimization_barrier((flats, rest))
    from_left, from_right, across_two = rest
    el = expand(same, across_two, from_left, from_right)
    matrix, el = lax.optimization_barrier((matrix, el))
    ec = shift(el, dc=1)
    *more, own = cut_matrix(where, matrix, MESSAGES[2:], ((late, 0),))
    far += more
    fars += [across(f) for f in far[1:3]]

    sums = [None, None]
    for s in range(Z):
        if s >= 2:
            fars[s - 1], total = lax.optimization_barrier((fars[s - 1], total))
            sums[1 - s % 2] = shift(total, dz=2 * (s % 2) - 1, mirror=True)
            cross = shift(fars[s - 1][1], dc=1)
            flats.append(flatten((own, (s - 2,)), (core, (s,)), (fars[s - 1], (0, 0)), (cross, (0,))))
        if s == Z - 1:
            total = term(el, ec, flats[s])
            break
        total = term(el, ec, flats[s], *sums[s % 2:s % 2 + 1] if s > 1 else ())
        if s in PACE:
            ahead, total = lax.optimization_barrier((far[len(fars) - 1], total))
            fars.append(across(ahead))
        if s == 0:
            flats[1], total = lax.optimization_barrier((flats[1], total))
            sums[0] = shift(total, dz=1, mirror=True)
    volume = finish(total, *sums)
    return volume.reshape(frames, parts, BR_DEV, -1)


def across(far):
    return shift(far, dx=1, mirror=True)


def solution(mesh):
    in_specs = (P("grp", None, None, "freq"), P("freq", None, None), P(), P())
    out_specs = P(None, None, "grp", "freq")
    return jax.shard_map(
        on_device, mesh=mesh, in_specs=in_specs, out_specs=out_specs, check_vma=False
    )
```
